128 devices in a mesh: sec: 2 (over core), tile: 64 (over y, x, z).
Axes of the slice: x: 4, y: 4, z: 4, core: 2. Of those that a mesh axis runs over, the one named last changes fastest.
Arguments:
- section_state: float32 [2, 72, 1048576], P('sec', None, 'tile'), may hold values from -6 to 6
- matrices: float32 [2, 72, 72], replicated, may hold values from -0.75 to 0.75
- blocks: bfloat16 [2, 16384, 128, 128], P('sec', 'tile'), may hold values from -0.5 to 0.5
- src_slot: int32 [2, 16384], P('sec', 'tile'), may hold values from 0 to 127
- dst_dev: int32 [2, 16384, 1], P('sec', 'tile'), may hold values from 0 to 63; in each aligned block of 256 rows (0 to 255, 256 to 511, ..., all dimensions but the last counted through in order) at most 8 rows name the same one
- dst_slot: int32 [2, 16384], P('sec', 'tile'), may hold values from 0 to 127
Outputs:
- new_state: float32 [2, 72, 1048576], P('sec', None, 'tile')
The draws below stay inside these ranges and needn't reach their ends.
Inputs may be any that keep to these rules, and one draw needn't show every extreme that they name: `dst_dev`: in the rows of one device (aligned blocks of 256 rows along the second dimension), no destination index occurs more than 8 times, and some index occurs exactly 8 times.
All inputs are finite; a program needn't handle non-finite values.
Results may differ from the reference program's by a relative error of at most 0.0015.
Values sent between devices are 32-bit elements; how exact they have to be, the bound alone decides.
A program may use at most 128 MiB of HBM per device.

```python
import math
import jax
import jax.numpy as jnp
import numpy as np
from jax import lax

LEV = 72
FIELDS = 8
TILES = 128
BLOCKS = 256
CAP = 8
SEC_TILES = 8192
CELLS = 1048576
N_TILE = 64


def with_ends(result, own_key, low, largest):
    place = [jax.random.randint(jax.random.fold_in(own_key, axis), (), 0, length) for axis, length in enumerate(result.shape)]
    longest = result.shape.index(max(result.shape))
    neighbour = place[:longest] + [(place[longest] + 1) % result.shape[longest]] + place[longest + 1:]
    return result.at[tuple(place)].set(low).at[tuple(neighbour)].set(largest)


def levels(key, extent, shards, least, largest):
    gain, own = 1.0, jax.random.fold_in(key, 6)
    for axis_at, shards_of in shards:
        steps = jnp.exp(jax.random.uniform(jax.random.fold_in(own, axis_at), (shards_of,), jnp.float32, least / len(shards), largest / len(shards)))
        gain = gain * jnp.repeat(steps, extent[axis_at] // shards_of).reshape([-1 if axis == axis_at else 1 for axis in range(len(extent))])
    return gain


def deal_out(stream_key, own, number, rows, number_of, top, bound, lean):
    ranking = jax.random.permutation(stream_key, number_of)
    crowded, usual = shares(number_of, rows * top, bound, lean, True), shares(number_of, rows * top, bound, lean, False)
    places = jnp.arange(number_of)

    def named(sizes, rotation):
        used = int((sizes > 0).sum())
        fixed = max(1, used // 4)
        moved = fixed + (places - fixed + rotation * (used - fixed)) % max(1, number_of - fixed)
        return jnp.zeros((number_of,), jnp.int32).at[ranking[jnp.where(places < fixed, places, moved)]].set(jnp.asarray(sizes, jnp.int32))

    sizes = jnp.where(number % 4 == 0, named(crowded, number // 4), named(usual, number - number // 4 - 1))
    mixed = jax.random.permutation(jax.random.fold_in(own, 3), number_of)
    source_of, receiver = mixed[0:number_of // 2 * 2:2], mixed[1:number_of // 2 * 2:2]
    room = jnp.minimum(sizes[source_of] - 1, bound - sizes[receiver]) // 2
    room = jnp.where((source_of == ranking[0]) | (receiver == ranking[0]) | (sizes[receiver] == 0), 0, jnp.maximum(room, 0))
    moved = jax.random.randint(jax.random.fold_in(own, 4), (number_of // 2,), 0, 1 << 20) % (room + 1)
    sizes = sizes.at[source_of].add(-moved).at[receiver].add(moved)
    members = jnp.searchsorted(jnp.cumsum(sizes), jnp.arange(rows * top), side="right").astype(jnp.int32)
    table = members.reshape(top, rows).T
    table = table[jax.random.permutation(jax.random.fold_in(own, 1), rows)]
    rotation = jax.random.randint(jax.random.fold_in(own, 2), (rows, 1), 0, top)
    return jnp.take_along_axis(table, (jnp.arange(top)[None, :] + rotation) % top, axis=1)


def shares(amount, total, reach, lean, full):
    portions = [(1 << 20) // math.isqrt(rank ** lean) + 1 for rank in range(1, amount + 1)]
    largest = reach if full else min(reach, max(-(-total // amount), total * portions[0] // sum(portions)))
    least = 1 if total - largest >= amount - 1 else 0
    holding, rest = [largest] + [least] * (amount - 1), total - largest - least * (amount - 1)
    while rest > 0:
        candidates = [i for i in range(1, amount) if holding[i] < largest] or [i for i in range(1, amount) if holding[i] < reach]
        mass, left = sum([portions[i] for i in candidates]), rest
        for i in candidates:
            extra = min(reach - holding[i], max(1, left * portions[i] // mass), rest)
            holding[i] = holding[i] + extra
            rest = rest - extra
    return np.array(holding)


def gaussian(rng, extent, width, limit, split=(), kind=jnp.bfloat16):
    level = levels(rng, extent, split, -0.22, 0.18) if split else 1.0
    drawn = jax.random.normal(rng, extent, jnp.float32) * width * level
    return jnp.minimum(jnp.maximum(drawn, -limit), limit).astype(kind)


def setup_inputs(seed: int = 0) -> dict:
    streams_of = jax.random.split(jax.random.key(seed), 7)
    section_state = gaussian(streams_of[0], (2, LEV, CELLS), 1.0, 6.0, ((0, 2), (2, 64)), jnp.float32)
    matrices = gaussian(streams_of[1], (2, LEV, LEV), LEV ** -0.5, 0.75, (), jnp.float32)
    blocks = gaussian(streams_of[2], (2, N_TILE * BLOCKS, 128, 128), 128 ** -0.5, 0.5, ((0, 2), (1, 64)))
    src_slot = with_ends(jax.random.randint(streams_of[3], (2, N_TILE * BLOCKS), 0, TILES), jax.random.fold_in(streams_of[3], 1), 0, TILES - 1).astype(jnp.int32)
    dst_dev_keys = jax.random.split(jax.random.fold_in(streams_of[4], 1), 2 * (N_TILE * BLOCKS) // BLOCKS)
    dst_dev_turns = jax.random.permutation(jax.random.fold_in(streams_of[4], 3), 2 * (N_TILE * BLOCKS) // BLOCKS)
    dst_dev = jax.vmap(lambda own, number: deal_out(jax.random.fold_in(streams_of[4], 2), own, number, BLOCKS, N_TILE, 1, CAP, 2))(dst_dev_keys, dst_dev_turns).reshape((2, N_TILE * BLOCKS, 1))
    dst_slot = with_ends(jax.random.randint(streams_of[5], (2, N_TILE * BLOCKS), 0, TILES), jax.random.fold_in(streams_of[5], 1), 0, TILES - 1).astype(jnp.int32)
    return {"section_state": section_state, "matrices": matrices, "blocks": blocks, "src_slot": src_slot, "dst_dev": dst_dev, "dst_slot": dst_slot}


step_weight = 0.5
atmos_visc = 0.22
ocean_visc = 0.24


def physics(field, matrix, count):
    for number in range(count):
        product = jnp.dot(matrix, field, precision=lax.Precision.HIGHEST, preferred_element_type=jnp.float32)
        field = field + step_weight * jnp.tanh(product)
    return field


def diffuse(field, visc):
    grid = field.reshape(LEV, SEC_TILES, 128)
    for number in range(4):
        padded = jnp.pad(grid, ((0, 0), (1, 1), (0, 0)))
        north = padded[:, :-2, :]
        south = padded[:, 2:, :]
        east = jnp.roll(grid, -1, axis=2)
        west = jnp.roll(grid, 1, axis=2)
        grid = grid + visc * (north + south + east + west - 4.0 * grid)
    return grid.reshape(LEV, CELLS)


def remap(export, weights, source_slot, dest_dev, dest_slot):
    owner = jnp.arange(N_TILE * BLOCKS, dtype=jnp.int32) // BLOCKS
    source = (owner * TILES + source_slot).astype(jnp.int32)
    target = (dest_dev[:, 0] * TILES + dest_slot).astype(jnp.int32)
    grouped = weights.reshape(N_TILE, BLOCKS, 128, 128)
    sources = source.reshape(N_TILE, BLOCKS)

    def group(items):
        weight_group, source_group = items
        picked = export[:, source_group, :].astype(jnp.float32)
        return jnp.einsum('bji,fbi->bfj', weight_group.astype(jnp.float32), picked)

    partial_value = lax.map(group, (grouped, sources))
    imported = jnp.zeros((SEC_TILES, FIELDS, 128), jnp.float32)
    imported = imported.at[target].add(partial_value.reshape(N_TILE * BLOCKS, FIELDS, 128))
    return jnp.transpose(imported, (1, 0, 2)).reshape(FIELDS, CELLS)


def reference(section_state, matrices, blocks, src_slot, dst_dev, dst_slot):
    atmos = section_state[0]
    ocean = section_state[1]
    atmos_export = atmos[LEV - FIELDS:].astype(jnp.bfloat16).reshape(FIELDS, SEC_TILES, 128)
    ocean_export = ocean[:FIELDS].astype(jnp.bfloat16).reshape(FIELDS, SEC_TILES, 128)
    to_ocean = remap(atmos_export, blocks[0], src_slot[0], dst_dev[0], dst_slot[0])
    to_atmos = remap(ocean_export, blocks[1], src_slot[1], dst_dev[1], dst_slot[1])
    atmos = atmos.at[LEV - FIELDS:].add(to_atmos)
    ocean = ocean.at[:FIELDS].add(to_ocean)
    atmos = physics(atmos, matrices[0], 2)
    ocean = physics(ocean, matrices[1], 1)
    atmos = diffuse(atmos, atmos_visc)
    ocean = diffuse(ocean, ocean_visc)
    return jnp.stack([atmos, ocean])
```

```python
import functools
import itertools
import random

import jax
import jax.numpy as jnp
from jax import lax
from jax.experimental import pallas as pl
from jax.experimental.pallas import tpu as pltpu
from jax.sharding import PartitionSpec as P

MESH = pl.DeviceIdType.MESH
FIELDS = 8
DEPTH = 8
LANES = 128
STEPS = 4
ATMOS_VISC = 0.22
OCEAN_VISC = 0.24


def torus(count):
    side = round(count ** (1 / 3))
    return (side, side, side)


def send_order(dims):
    offsets = list(itertools.product(*[range(n) for n in dims]))
    random.Random(1).shuffle(offsets)

    def hops(offset):
        return sum(min(a, n - a) for a, n in zip(offset, dims))

    return sorted(offsets, key=lambda offset: -hops(offset))


def split(value):
    high = value.astype(jnp.bfloat16).astype(jnp.float32)
    return high, value - high


def stacked(value):
    high, low = split(value)
    return jnp.concatenate([high, low, high], axis=0).astype(jnp.bfloat16)


def weights(matrix):
    high, low = split(matrix)
    return jnp.concatenate([high, high, low], axis=1).astype(jnp.bfloat16)


def column(row):
    return jnp.transpose(jnp.broadcast_to(row, (8, row.shape[1])))[:, :1]


def exchange(
    dims,
    state_hbm,
    mats,
    blocks_hbm,
    src_slot,
    dst_dev,
    dst_slot,
    out_hbm,
    north_hbm,
    south_hbm,
    blocks_v,
    export_v,
    cells_v,
    part_v,
    out_v,
    recv_v,
    meta_v,
    meta_r,
    x_v,
    p_v,
    imp_v,
    place_v,
    place_s,
    load_sem,
    place_sem,
    send_sem,
    recv_sem,
    msend_sem,
    mrecv_sem,
    hsend_sem,
    hrecv_sem,
    store_sem,
):
    levels, cells = x_v.shape
    tiles = cells // LANES
    blocks = blocks_v.shape[0]
    peers = dims[0] * dims[1] * dims[2]
    order = send_order(dims)
    section = lax.axis_index("sec")
    me = lax.axis_index("tile")
    other = 1 - section
    y, x, z = me // (dims[1] * dims[2]), (me // dims[2]) % dims[1], me % dims[2]

    def at(offset, sign):
        dy, dx, dz = offset
        ny, nx, nz = dims
        return (
            ((y + ny + sign * dy) % ny) * (nx * nz)
            + ((x + nx + sign * dx) % nx) * nz
            + (z + nz + sign * dz) % nz
        )

    after, before = (me + 1) % peers, (me + peers - 1) % peers

    start = other * (levels - FIELDS)
    get_export = pltpu.make_async_copy(state_hbm.at[pl.ds(start, FIELDS)], export_v, load_sem.at[0])
    get_export.start()
    chunks = 8
    per = blocks // chunks
    get_blocks = []
    for c in range(chunks):
        get = pltpu.make_async_copy(
            blocks_hbm.at[pl.ds(c * per, per)], blocks_v.at[pl.ds(c * per, per)], load_sem.at[1 + c]
        )
        get.start()
        get_blocks.append(get)
    get_state = pltpu.make_async_copy(state_hbm, x_v, load_sem.at[1 + chunks])
    get_state.start()

    barrier = pltpu.get_barrier_semaphore()
    for offset in order:
        pl.semaphore_signal(barrier, inc=1, device_id=(other, at(offset, -1)), device_id_type=MESH)
    for side in (before, after):
        pl.semaphore_signal(barrier, inc=1, device_id=(section, side), device_id_type=MESH)

    owner = dst_dev[...]
    earlier = lax.broadcasted_iota(jnp.int32, (blocks, blocks), 0) < lax.broadcasted_iota(
        jnp.int32, (blocks, blocks), 1
    )
    alike = earlier & (column(owner) == owner)
    position = owner * DEPTH + jnp.sum(jnp.where(alike, 1, 0), axis=0, keepdims=True)
    fills = column(position) == lax.broadcasted_iota(jnp.int32, (blocks, peers * DEPTH), 1)
    number = lax.broadcasted_iota(jnp.int32, (blocks, peers * DEPTH), 0)
    place_v[0:1, :] = jnp.sum(jnp.where(fills, number, 0), axis=0, keepdims=True)
    place_v[1:2, :] = jnp.sum(jnp.where(fills, column(dst_slot[...]) + 1, 0), axis=0, keepdims=True)
    get_place = pltpu.make_async_copy(place_v, place_s, place_sem)
    get_place.start()

    get_export.wait()
    for tile in range(tiles):
        cells_v[tile] = export_v[:, tile * LANES : (tile + 1) * LANES]
    for c in range(chunks):
        get_blocks[c].wait()

        def remap(i, carry, c=c):
            for u in range(8):
                b = c * per + i * 8 + u
                tile = src_slot[0, b]
                part_v[b] = lax.dot_general(
                    cells_v[tile].astype(jnp.bfloat16),
                    blocks_v[b],
                    (((1,), (1,)), ((), ())),
                    preferred_element_type=jnp.float32,
                )
            return carry

        lax.fori_loop(0, per // 8, remap, 0)

    get_place.wait()
    pl.semaphore_wait(barrier, peers + 2)

    rows = DEPTH * FIELDS
    lane = lax.broadcasted_iota(jnp.int32, (1, LANES), 1)
    group = LANES // DEPTH
    data, meta = [], []
    for k, offset in enumerate(order):
        dest = at(offset, 1)
        line = jnp.zeros((1, LANES), jnp.int32)
        for r in range(DEPTH):
            b = place_s[0, dest * DEPTH + r]
            out_v[pl.ds(k * rows + r * FIELDS, FIELDS), :] = part_v[b]
            line = jnp.where(lane == (k % group) * DEPTH + r, place_s[1, dest * DEPTH + r], line)
        meta_v[k] = line.astype(jnp.float32)
        target = (other, dest)
        copy = pltpu.make_async_remote_copy(
            src_ref=out_v.at[pl.ds(k * rows, rows)],
            dst_ref=recv_v.at[pl.ds(k * rows, rows)],
            send_sem=send_sem.at[k],
            recv_sem=recv_sem.at[k],
            device_id=target,
            device_id_type=MESH,
        )
        copy.start()
        data.append(copy)
        copy = pltpu.make_async_remote_copy(
            src_ref=meta_v.at[k],
            dst_ref=meta_r.at[k],
            send_sem=msend_sem.at[k],
            recv_sem=mrecv_sem.at[k],
            device_id=target,
            device_id_type=MESH,
        )
        copy.start()
        meta.append(copy)

    matrix = mats[section]
    full = weights(matrix)
    edge = weights(jnp.where(section == 0, matrix[:, levels - FIELDS :], matrix[:, :FIELDS]))
    width = 512
    get_state.wait()

    def ahead(i, carry):
        cols = pl.ds(pl.multiple_of(i * width, width), width)
        p_v[:, cols] = jnp.dot(full, stacked(x_v[:, cols]), preferred_element_type=jnp.float32)
        return carry

    lax.fori_loop(0, cells // width, ahead, 0)

    tile_number = lax.broadcasted_iota(jnp.int32, (tiles, LANES), 0).astype(jnp.float32)
    for q in range(peers // group):
        line = jnp.zeros((1, LANES), jnp.float32)
        for k in range(q * group, (q + 1) * group):
            meta[k].wait_recv()
            line = line + meta_r[k]
            data[k].wait_recv()
        chosen = (tile_number == line - 1.0).astype(jnp.float32)
        chosen = jnp.concatenate([chosen, chosen], axis=1).astype(jnp.bfloat16)
        for f in range(FIELDS):
            value = recv_v[pl.ds(q * group * rows + f, group * DEPTH, stride=FIELDS), :]
            high, low = split(value)
            term = jnp.dot(
                chosen,
                jnp.concatenate([high, low], axis=0).astype(jnp.bfloat16),
                preferred_element_type=jnp.float32,
            )
            to = pl.ds(f, tiles, stride=FIELDS)
            if q == 0:
                imp_v[to, :] = term
            else:
                imp_v[to, :] = imp_v[to, :] + term

    per_width = width // LANES

    def columns(i, substeps):
        cols = pl.ds(pl.multiple_of(i * width, width), width)
        imported = jnp.concatenate(
            [
                imp_v[pl.ds(pl.multiple_of((i * per_width + j) * FIELDS, FIELDS), FIELDS), :]
                for j in range(per_width)
            ],
            axis=1,
        )
        x_v[pl.ds(start, FIELDS), cols] = x_v[pl.ds(start, FIELDS), cols] + imported
        product = p_v[:, cols] + jnp.dot(edge, stacked(imported), preferred_element_type=jnp.float32)
        value = x_v[:, cols] + 0.5 * jnp.tanh(product)
        if substeps == 2:
            product = jnp.dot(full, stacked(value), preferred_element_type=jnp.float32)
            value = value + 0.5 * jnp.tanh(product)
        x_v[:, cols] = value

    halo = STEPS * LANES
    last = cells // width - 1

    def both(i):
        @pl.when(section == 0)
        def _():
            columns(i, 2)

        @pl.when(section == 1)
        def _():
            columns(i, 1)

    both(0)
    both(last)
    to_before = pltpu.make_async_remote_copy(
        src_ref=x_v.at[:, pl.ds(0, halo)],
        dst_ref=south_hbm,
        send_sem=hsend_sem.at[0],
        recv_sem=hrecv_sem.at[0],
        device_id=(section, before),
        device_id_type=MESH,
    )
    to_after = pltpu.make_async_remote_copy(
        src_ref=x_v.at[:, pl.ds(cells - halo, halo)],
        dst_ref=north_hbm,
        send_sem=hsend_sem.at[1],
        recv_sem=hrecv_sem.at[1],
        device_id=(section, after),
        device_id_type=MESH,
    )
    to_before.start()
    to_after.start()
    pieces = 4
    span = cells // pieces
    stores = []
    for piece in range(pieces):
        low = max(1, piece * span // width)
        high = min(last, (piece + 1) * span // width)

        @pl.when(section == 0)
        def _(low=low, high=high):
            lax.fori_loop(low, high, lambda i, carry: (columns(i, 2), carry)[1], 0)

        @pl.when(section == 1)
        def _(low=low, high=high):
            lax.fori_loop(low, high, lambda i, carry: (columns(i, 1), carry)[1], 0)

        store = pltpu.make_async_copy(
            x_v.at[:, pl.ds(piece * span, span)], out_hbm.at[:, pl.ds(piece * span, span)], store_sem.at[piece]
        )
        store.start()
        stores.append(store)
    for copy in data + meta:
        copy.wait_send()
    for store in stores:
        store.wait()
    for copy in (to_before, to_after):
        copy.wait()


def diffuse(x_ref, north_ref, south_ref, o_ref):
    levels, cells = x_ref.shape
    rows = cells // LANES
    streams = levels // 8
    section = lax.axis_index("sec")
    me = lax.axis_index("tile")
    peers = lax.axis_size("tile")
    visc = jnp.where(section == 0, ATMOS_VISC, OCEAN_VISC).astype(jnp.float32)
    center = (1.0 - 4.0 * visc) / visc
    scale = (visc * visc) * (visc * visc)
    top = jnp.where(me == 0, 0.0, 1.0).astype(jnp.float32)
    bottom = jnp.where(me == peers - 1, 0.0, 1.0).astype(jnp.float32)

    def advance(new, carry, masks):
        out = []
        for s in range(streams):
            value = new[s]
            kept = []
            for k in range(STEPS):
                part, prior = carry[s][k]
                if masks[k] is not None:
                    value = value * masks[k]
                fresh = (
                    center * value
                    + (pltpu.roll(value, 1, 1) + pltpu.roll(value, LANES - 1, 1))
                    + prior
                )
                kept.append((fresh, value))
                value = part + value
            out.append((value, tuple(kept)))
        return [v for v, _ in out], tuple(k for _, k in out)

    zero = jnp.zeros((8, LANES), jnp.float32)
    carry = tuple(tuple((zero, zero) for _ in range(STEPS)) for _ in range(streams))

    def load(ref, row):
        at = row * LANES if isinstance(row, int) else pl.multiple_of(row * LANES, LANES)
        return [ref[pl.ds(8 * s, 8), pl.ds(at, LANES)] for s in range(streams)]

    def store(row, values):
        at = row * LANES if isinstance(row, int) else pl.multiple_of(row * LANES, LANES)
        for s in range(streams):
            o_ref[0, pl.ds(8 * s, 8), pl.ds(at, LANES)] = values[s] * scale

    def masks_at(row):
        return [top if row - k < 0 else (bottom if row - k >= rows else None) for k in range(STEPS)]

    for row in range(-STEPS, STEPS):
        new = load(north_ref, row + STEPS) if row < 0 else load(x_ref, row)
        _, carry = advance(new, carry, masks_at(row))

    unroll = 4

    def body(i, carry):
        for u in range(unroll):
            row = STEPS + i * unroll + u
            values, carry = advance(load(x_ref, row), carry, [None] * STEPS)
            store(row - STEPS, values)
        return carry

    carry = lax.fori_loop(0, (rows - STEPS) // unroll, body, carry)
    for row in range(rows, rows + STEPS):
        values, carry = advance(load(south_ref, row - rows), carry, masks_at(row))
        store(row - STEPS, values)


def per_device(dims, section_state, matrices, blocks, src_slot, dst_dev, dst_slot):
    _, levels, cells = section_state.shape
    block_count = blocks.shape[1]
    tiles = cells // LANES
    peers = dims[0] * dims[1] * dims[2]
    halo = STEPS * LANES
    f32, i32, dma = jnp.float32, jnp.int32, pltpu.SemaphoreType.DMA
    anywhere = pl.BlockSpec(memory_space=pl.ANY)
    vmem = pl.BlockSpec(memory_space=pltpu.VMEM)
    slots = peers * DEPTH * FIELDS
    state, north, south = pl.pallas_call(
        functools.partial(exchange, dims),
        out_shape=[
            jax.ShapeDtypeStruct((levels, cells), f32),
            jax.ShapeDtypeStruct((levels, halo), f32),
            jax.ShapeDtypeStruct((levels, halo), f32),
        ],
        in_specs=[anywhere, vmem, anywhere, pl.BlockSpec(memory_space=pltpu.SMEM), vmem, vmem],
        out_specs=[anywhere, anywhere, anywhere],
        scratch_shapes=[
            pltpu.VMEM((block_count, LANES, LANES), jnp.bfloat16),
            pltpu.VMEM((FIELDS, cells), f32),
            pltpu.VMEM((tiles, FIELDS, LANES), f32),
            pltpu.VMEM((block_count, FIELDS, LANES), f32),
            pltpu.VMEM((slots, LANES), f32),
            pltpu.VMEM((slots, LANES), f32),
            pltpu.VMEM((peers, 1, LANES), f32),
            pltpu.VMEM((peers, 1, LANES), f32),
            pltpu.VMEM((levels, cells), f32),
            pltpu.VMEM((levels, cells), f32),
            pltpu.VMEM((tiles * FIELDS, LANES), f32),
            pltpu.VMEM((8, peers * DEPTH), i32),
            pltpu.SMEM((8, peers * DEPTH), i32),
            dma((10,)),
            dma,
            dma((peers,)),
            dma((peers,)),
            dma((peers,)),
            dma((peers,)),
            dma((2,)),
            dma((2,)),
            dma((4,)),
        ],
        compiler_params=pltpu.CompilerParams(
            collective_id=0, has_side_effects=True, vmem_limit_bytes=48 << 20
        ),
    )(
        section_state.reshape(levels, cells),
        matrices,
        blocks.reshape(block_count, LANES, LANES),
        src_slot,
        dst_dev.reshape(1, block_count),
        dst_slot,
    )
    band = 24
    return pl.pallas_call(
        diffuse,
        grid=(levels // band,),
        out_shape=jax.ShapeDtypeStruct((1, levels, cells), f32),
        in_specs=[
            pl.BlockSpec((band, cells), lambda i: (i, 0)),
            pl.BlockSpec((band, halo), lambda i: (i, 0)),
            pl.BlockSpec((band, halo), lambda i: (i, 0)),
        ],
        out_specs=pl.BlockSpec((1, band, cells), lambda i: (0, i, 0)),
        compiler_params=pltpu.CompilerParams(vmem_limit_bytes=32 << 20),
    )(state, north, south)


def solution(mesh):
    in_specs = (
        P("sec", None, "tile"),
        P(),
        P("sec", "tile", None, None),
        P("sec", "tile"),
        P("sec", "tile", None),
        P("sec", "tile"),
    )
    return jax.shard_map(
        functools.partial(per_device, torus(mesh.shape["tile"])),
        mesh=mesh,
        in_specs=in_specs,
        out_specs=P("sec", None, "tile"),
        check_vma=False,
    )
```

```python
import functools
import itertools
import random

import jax
import jax.numpy as jnp
from jax import lax
from jax.experimental import pallas as pl
from jax.experimental.pallas import tpu as pltpu
from jax.sharding import PartitionSpec as P

MESH = pl.DeviceIdType.MESH
FIELDS = 8
DEPTH = 8
LANES = 128
STEPS = 4
ATMOS_VISC = 0.22
OCEAN_VISC = 0.24
VMEM_BYTES = 60 << 20


def torus(count):
    side = round(count ** (1 / 3))
    return (side, side, side)


def send_order(dims):
    offsets = list(itertools.product(*[range(n) for n in dims]))
    random.Random(1).shuffle(offsets)

    def hops(offset):
        return sum(min(a, n - a) for a, n in zip(offset, dims))

    return sorted(offsets, key=lambda offset: -hops(offset))


def split(value):
    high = value.astype(jnp.bfloat16).astype(jnp.float32)
    return high, value - high


def stacked(value):
    high, low = split(value)
    return jnp.concatenate([high, low, high], axis=0).astype(jnp.bfloat16)


def weights(matrix):
    high, low = split(matrix)
    return jnp.concatenate([high, high, low], axis=1).astype(jnp.bfloat16)


def column(row):
    return jnp.transpose(jnp.broadcast_to(row, (8, row.shape[1])))[:, :1]


def exchange(
    dims,
    state_hbm,
    mats,
    blocks_hbm,
    src_slot,
    dst_dev,
    dst_slot,
    out_hbm,
    north_hbm,
    south_hbm,
    blocks_v,
    export_v,
    cells_v,
    part_v,
    out_v,
    recv_v,
    meta_v,
    meta_r,
    x_v,
    p_v,
    imp_v,
    place_v,
    place_s,
    load_sem,
    place_sem,
    send_sem,
    recv_sem,
    msend_sem,
    mrecv_sem,
    hsend_sem,
    hrecv_sem,
    store_sem,
):
    levels, cells = x_v.shape
    tiles = cells // LANES
    blocks = blocks_v.shape[0]
    peers = dims[0] * dims[1] * dims[2]
    order = send_order(dims)
    section = lax.axis_index("sec")
    me = lax.axis_index("tile")
    other = 1 - section
    y, x, z = me // (dims[1] * dims[2]), (me // dims[2]) % dims[1], me % dims[2]

    def at(offset, sign):
        dy, dx, dz = offset
        ny, nx, nz = dims
        return (
            ((y + ny + sign * dy) % ny) * (nx * nz)
            + ((x + nx + sign * dx) % nx) * nz
            + (z + nz + sign * dz) % nz
        )

    after, before = (me + 1) % peers, (me + peers - 1) % peers

    start = other * (levels - FIELDS)
    get_export = pltpu.make_async_copy(state_hbm.at[pl.ds(start, FIELDS)], export_v, load_sem.at[0])
    get_export.start()
    chunks = 8
    per = blocks // chunks

    def get_blocks(c):
        part = pl.ds(c * per, per)
        return pltpu.make_async_copy(blocks_hbm.at[part], blocks_v.at[part], load_sem.at[1 + c])

    for c in range(chunks):
        get_blocks(c).start()

    barrier = pltpu.get_barrier_semaphore()
    for offset in order:
        pl.semaphore_signal(barrier, inc=1, device_id=(other, at(offset, -1)), device_id_type=MESH)
    for side in (before, after):
        pl.semaphore_signal(barrier, inc=1, device_id=(section, side), device_id_type=MESH)

    owner = dst_dev[...]
    earlier = lax.broadcasted_iota(jnp.int32, (blocks, blocks), 0) < lax.broadcasted_iota(
        jnp.int32, (blocks, blocks), 1
    )
    alike = earlier & (column(owner) == owner)
    position = owner * DEPTH + jnp.sum(jnp.where(alike, 1, 0), axis=0, keepdims=True)
    fills = column(position) == lax.broadcasted_iota(jnp.int32, (blocks, peers * DEPTH), 1)
    number = lax.broadcasted_iota(jnp.int32, (blocks, peers * DEPTH), 0)
    place_v[0:1, :] = jnp.sum(jnp.where(fills, number, 0), axis=0, keepdims=True)
    place_v[1:2, :] = jnp.sum(jnp.where(fills, column(dst_slot[...]) + 1, 0), axis=0, keepdims=True)
    get_place = pltpu.make_async_copy(place_v, place_s, place_sem)
    get_place.start()

    get_export.wait()
    for tile in range(tiles):
        cells_v[tile] = export_v[:, tile * LANES : (tile + 1) * LANES]

    def remap(c, carry):
        get_blocks(c).wait()
        for u in range(0, per, 2):
            b = c * per + u
            cell = jnp.concatenate([cells_v[src_slot[0, b]], cells_v[src_slot[0, b + 1]]], axis=0)
            both = lax.dot_general(
                cell.astype(jnp.bfloat16),
                blocks_v[pl.ds(b, 2)].reshape(2 * LANES, LANES),
                (((1,), (1,)), ((), ())),
                preferred_element_type=jnp.float32,
            )
            part_v[b] = both[:FIELDS, :LANES]
            part_v[b + 1] = both[FIELDS:, LANES:]
        return carry

    lax.fori_loop(0, chunks, remap, 0)
    get_state = pltpu.make_async_copy(state_hbm, x_v, load_sem.at[1 + chunks])
    get_state.start()
    get_place.wait()
    pl.semaphore_wait(barrier, peers + 2)

    rows = DEPTH * FIELDS
    lane = lax.broadcasted_iota(jnp.int32, (1, LANES), 1)
    group = LANES // DEPTH
    data, meta = [], []
    for k, offset in enumerate(order):
        dest = at(offset, 1)
        line = jnp.zeros((1, LANES), jnp.int32)
        for r in range(DEPTH):
            b = place_s[0, dest * DEPTH + r]
            out_v[pl.ds(k * rows + r * FIELDS, FIELDS), :] = part_v[b]
            line = jnp.where(lane == (k % group) * DEPTH + r, place_s[1, dest * DEPTH + r], line)
        meta_v[k] = line.astype(jnp.float32)
        target = (other, dest)
        copy = pltpu.make_async_remote_copy(
            src_ref=out_v.at[pl.ds(k * rows, rows)],
            dst_ref=recv_v.at[pl.ds(k * rows, rows)],
            send_sem=send_sem.at[k],
            recv_sem=recv_sem.at[k],
            device_id=target,
            device_id_type=MESH,
        )
        copy.start()
        data.append(copy)
        copy = pltpu.make_async_remote_copy(
            src_ref=meta_v.at[k],
            dst_ref=meta_r.at[k],
            send_sem=msend_sem.at[k],
            recv_sem=mrecv_sem.at[k],
            device_id=target,
            device_id_type=MESH,
        )
        copy.start()
        meta.append(copy)

    matrix = mats[section]
    full = weights(matrix)
    edge = weights(jnp.where(section == 0, matrix[:, levels - FIELDS :], matrix[:, :FIELDS]))
    width = 512
    get_state.wait()

    def ahead(i, carry):
        cols = pl.ds(pl.multiple_of(i * width, width), width)
        p_v[:, cols] = jnp.dot(full, stacked(x_v[:, cols]), preferred_element_type=jnp.float32)
        return carry

    lax.fori_loop(0, cells // width, ahead, 0)

    tile_number = lax.broadcasted_iota(jnp.int32, (tiles, LANES), 0).astype(jnp.float32)
    for q in range(peers // group):
        line = jnp.zeros((1, LANES), jnp.float32)
        for k in range(q * group, (q + 1) * group):
            meta[k].wait_recv()
            line = line + meta_r[k]
            data[k].wait_recv()
        chosen = (tile_number == line - 1.0).astype(jnp.float32)
        chosen = jnp.concatenate([chosen, chosen], axis=1).astype(jnp.bfloat16)
        for f in range(FIELDS):
            value = recv_v[pl.ds(q * group * rows + f, group * DEPTH, stride=FIELDS), :]
            high, low = split(value)
            term = jnp.dot(
                chosen,
                jnp.concatenate([high, low], axis=0).astype(jnp.bfloat16),
                preferred_element_type=jnp.float32,
            )
            to = pl.ds(f, tiles, stride=FIELDS)
            if q == 0:
                imp_v[to, :] = term
            else:
                imp_v[to, :] = imp_v[to, :] + term

    width = 2048
    chunks = cells // width
    per_width = width // LANES

    def put(i):
        cols = pl.ds(pl.multiple_of(i * width, width), width)
        return pltpu.make_async_copy(x_v.at[:, cols], out_hbm.at[:, cols], store_sem.at[i])

    def columns(substeps, i, carry):
        i = (i + chunks - 1) % chunks
        cols = pl.ds(pl.multiple_of(i * width, width), width)
        imported = jnp.concatenate(
            [
                imp_v[pl.ds(pl.multiple_of((i * per_width + j) * FIELDS, FIELDS), FIELDS), :]
                for j in range(per_width)
            ],
            axis=1,
        )
        x_v[pl.ds(start, FIELDS), cols] = x_v[pl.ds(start, FIELDS), cols] + imported
        product = p_v[:, cols] + jnp.dot(edge, stacked(imported), preferred_element_type=jnp.float32)
        value = x_v[:, cols] + 0.5 * jnp.tanh(product)
        if substeps == 2:
            product = jnp.dot(full, stacked(value), preferred_element_type=jnp.float32)
            value = value + 0.5 * jnp.tanh(product)
        x_v[:, cols] = value
        put(i).start()
        return carry

    def physics(low, high):
        for number in range(2):

            @pl.when(section == number)
            def _(number=number):
                lax.fori_loop(low, high, functools.partial(columns, 2 - number), 0)

    physics(0, 2)
    halo = STEPS * LANES
    to_before = pltpu.make_async_remote_copy(
        src_ref=x_v.at[:, pl.ds(0, halo)],
        dst_ref=south_hbm,
        send_sem=hsend_sem.at[0],
        recv_sem=hrecv_sem.at[0],
        device_id=(section, before),
        device_id_type=MESH,
    )
    to_after = pltpu.make_async_remote_copy(
        src_ref=x_v.at[:, pl.ds(cells - halo, halo)],
        dst_ref=north_hbm,
        send_sem=hsend_sem.at[1],
        recv_sem=hrecv_sem.at[1],
        device_id=(section, after),
        device_id_type=MESH,
    )
    to_before.start()
    to_after.start()
    physics(2, chunks)
    for copy in data + meta:
        copy.wait_send()
    for i in range(chunks):
        put(i).wait()
    for copy in (to_before, to_after):
        copy.wait()


def ring_powers():
    shape = (2 * LANES, LANES)
    apart = (
        lax.broadcasted_iota(jnp.int32, shape, 0) + 2 * LANES - lax.broadcasted_iota(jnp.int32, shape, 1)
    ) % LANES
    terms = []
    for entries in ({1: 4}, {0: 12, 2: 6}, {1: 12, 3: 4}, {0: 6, 2: 4, 4: 1}):
        term = jnp.zeros(shape, jnp.float32)
        for distance, weight in entries.items():
            near = (apart == distance) | (apart == (LANES - distance) % LANES)
            term = jnp.where(near, float(weight), term)
        terms.append(term.astype(jnp.bfloat16))
    return jnp.concatenate(terms, axis=1)


def diffuse(x_ref, north_ref, south_ref, o_ref, coef_ref, side_ref):
    levels, cells = x_ref.shape
    rows = cells // LANES
    streams = levels // 8
    chunk = 32
    first = 2 * STEPS
    section = lax.axis_index("sec")
    me = lax.axis_index("tile")
    peers = lax.axis_size("tile")
    visc = jnp.where(section == 0, ATMOS_VISC, OCEAN_VISC).astype(jnp.float32)
    center = (1.0 - 4.0 * visc) / visc
    scale = (visc * visc) * (visc * visc)
    top = jnp.where(me == 0, 0.0, 1.0).astype(jnp.float32)
    bottom = jnp.where(me == peers - 1, 0.0, 1.0).astype(jnp.float32)

    @pl.when(pl.program_id(0) == 0)
    def _():
        coef_ref[...] = ring_powers()

    coef = coef_ref[...]

    def at(row):
        return row * LANES if isinstance(row, int) else pl.multiple_of(row * LANES, LANES)

    def load(ref, row):
        return [ref[pl.ds(8 * s, 8), pl.ds(at(row), LANES)] for s in range(streams)]

    def store(row, values):
        for s in range(streams):
            o_ref[0, pl.ds(8 * s, 8), pl.ds(at(row), LANES)] = values[s] * scale

    def sides(ref, row, count, place):
        value = jnp.concatenate([v for i in range(count) for v in load(ref, row + i)], axis=0)
        high = value.astype(jnp.bfloat16)
        low = (value - high.astype(jnp.float32)).astype(jnp.bfloat16)
        terms = jnp.dot(
            jnp.concatenate([high, low], axis=1), coef, preferred_element_type=jnp.float32
        )
        for i in range(count):
            for s in range(streams):
                m = (i * streams + s) * 8
                for k in range(STEPS):
                    side_ref[place + i, s, k] = terms[m : m + 8, k * LANES : (k + 1) * LANES]

    def advance(new, carry, row, edges):
        values, kept = [], []
        for s in range(streams):
            value, parts = new[s], []
            for k in range(STEPS):
                part, prior = carry[s][k]
                if edges and row - k < 0:
                    value = value * top
                if edges and row - k >= rows:
                    value = value * bottom
                parts.append((center * value + (side_ref[first + row - k, s, k] + prior), value))
                value = part + value
            values.append(value)
            kept.append(tuple(parts))
        return values, tuple(kept)

    zero = jnp.zeros((8, LANES), jnp.float32)
    carry = tuple(tuple((zero, zero) for _ in range(STEPS)) for _ in range(streams))
    for row in range(STEPS):
        for s in range(streams):
            for k in range(STEPS):
                side_ref[row, s, k] = zero
    sides(north_ref, 0, STEPS, first - STEPS)
    sides(x_ref, 0, chunk, first)
    for row in range(-STEPS, 0):
        _, carry = advance(load(north_ref, row + STEPS), carry, row, True)

    def several(i, carry, start=0, edges=False):
        for u in range(start, chunk):
            row = i * chunk + u
            values, carry = advance(load(x_ref, row), carry, row, edges)
            store(row - STEPS, values)
        return carry

    for row in range(STEPS):
        _, carry = advance(load(x_ref, row), carry, row, True)
    sides(x_ref, chunk, chunk, first + chunk)
    carry = several(0, carry, STEPS)

    def body(i, carry):
        sides(x_ref, (i + 1) * chunk, chunk, first + (i + 1) * chunk)
        return several(i, carry)

    last = rows // chunk - 1
    carry = lax.fori_loop(1, last, body, carry)
    sides(south_ref, 0, STEPS, first + rows)
    carry = several(last, carry)
    for row in range(rows, rows + STEPS):
        values, carry = advance(load(south_ref, row - rows), carry, row, True)
        store(row - STEPS, values)


def per_device(dims, section_state, matrices, blocks, src_slot, dst_dev, dst_slot):
    _, levels, cells = section_state.shape
    block_count = blocks.shape[1]
    tiles = cells // LANES
    peers = dims[0] * dims[1] * dims[2]
    halo = STEPS * LANES
    f32, i32, dma = jnp.float32, jnp.int32, pltpu.SemaphoreType.DMA
    anywhere = pl.BlockSpec(memory_space=pl.ANY)
    vmem = pl.BlockSpec(memory_space=pltpu.VMEM)
    slots = peers * DEPTH * FIELDS
    state, north, south = pl.pallas_call(
        functools.partial(exchange, dims),
        out_shape=[
            jax.ShapeDtypeStruct((levels, cells), f32),
            jax.ShapeDtypeStruct((levels, halo), f32),
            jax.ShapeDtypeStruct((levels, halo), f32),
        ],
        in_specs=[anywhere, vmem, anywhere, pl.BlockSpec(memory_space=pltpu.SMEM), vmem, vmem],
        out_specs=[anywhere, anywhere, anywhere],
        scratch_shapes=[
            pltpu.VMEM((block_count, LANES, LANES), jnp.bfloat16),
            pltpu.VMEM((FIELDS, cells), f32),
            pltpu.VMEM((tiles, FIELDS, LANES), f32),
            pltpu.VMEM((block_count, FIELDS, LANES), f32),
            pltpu.VMEM((slots, LANES), f32),
            pltpu.VMEM((slots, LANES), f32),
            pltpu.VMEM((peers, 1, LANES), f32),
            pltpu.VMEM((peers, 1, LANES), f32),
            pltpu.VMEM((levels, cells), f32),
            pltpu.VMEM((levels, cells), f32),
            pltpu.VMEM((tiles * FIELDS, LANES), f32),
            pltpu.VMEM((8, peers * DEPTH), i32),
            pltpu.SMEM((8, peers * DEPTH), i32),
            dma((10,)),
            dma,
            dma((peers,)),
            dma((peers,)),
            dma((peers,)),
            dma((peers,)),
            dma((2,)),
            dma((2,)),
            dma((8,)),
        ],
        compiler_params=pltpu.CompilerParams(
            collective_id=0, has_side_effects=True, vmem_limit_bytes=VMEM_BYTES
        ),
    )(
        section_state.reshape(levels, cells),
        matrices,
        blocks.reshape(block_count, LANES, LANES),
        src_slot,
        dst_dev.reshape(1, block_count),
        dst_slot,
    )
    band = 24
    return pl.pallas_call(
        diffuse,
        grid=(levels // band,),
        out_shape=jax.ShapeDtypeStruct((1, levels, cells), f32),
        in_specs=[
            pl.BlockSpec((band, cells), lambda i: (i, 0)),
            pl.BlockSpec((band, halo), lambda i: (i, 0)),
            pl.BlockSpec((band, halo), lambda i: (i, 0)),
        ],
        out_specs=pl.BlockSpec((1, band, cells), lambda i: (0, i, 0)),
        scratch_shapes=[
            pltpu.VMEM((2 * LANES, STEPS * LANES), jnp.bfloat16),
            pltpu.VMEM((cells // LANES + 3 * STEPS, band // 8, STEPS, 8, LANES), f32),
        ],
        compiler_params=pltpu.CompilerParams(vmem_limit_bytes=VMEM_BYTES),
    )(state, north, south)


def solution(mesh):
    in_specs = (
        P("sec", None, "tile"),
        P(),
        P("sec", "tile", None, None),
        P("sec", "tile"),
        P("sec", "tile", None),
        P("sec", "tile"),
    )
    return jax.shard_map(
        functools.partial(per_device, torus(mesh.shape["tile"])),
        mesh=mesh,
        in_specs=in_specs,
        out_specs=P("sec", None, "tile"),
        check_vma=False,
    )
```

```python
import functools
import itertools
import random

import jax
import jax.numpy as jnp
from jax import lax
from jax.experimental import pallas as pl
from jax.experimental.pallas import tpu as pltpu
from jax.sharding import PartitionSpec as P

MESH = pl.DeviceIdType.MESH
FIELDS = 8
DEPTH = 8
LANES = 128
STEPS = 4
HALF = 2
ATMOS_VISC = 0.22
OCEAN_VISC = 0.24
VMEM_BYTES = 60 << 20


def torus(count):
    side = round(count ** (1 / 3))
    return (side, side, side)


def send_order(dims):
    offsets = list(itertools.product(*[range(n) for n in dims]))
    random.Random(1).shuffle(offsets)

    def hops(offset):
        return sum(min(a, n - a) for a, n in zip(offset, dims))

    return sorted(offsets, key=lambda offset: -hops(offset))


def split(value):
    high = value.astype(jnp.bfloat16).astype(jnp.float32)
    return high, value - high


def stacked(value):
    high, low = split(value)
    return jnp.concatenate([high, low, high], axis=0).astype(jnp.bfloat16)


def weights(matrix):
    high, low = split(matrix)
    return jnp.concatenate([high, high, low], axis=1).astype(jnp.bfloat16)


def column(row):
    return jnp.transpose(jnp.broadcast_to(row, (8, row.shape[1])))[:, :1]


def exchange(
    dims,
    state_hbm,
    mats,
    blocks_hbm,
    src_slot,
    dst_dev,
    dst_slot,
    out_hbm,
    blocks_v,
    export_v,
    cells_v,
    part_v,
    out_v,
    recv_v,
    meta_v,
    meta_r,
    x_v,
    p_v,
    imp_v,
    north_v,
    south_v,
    coef_v,
    place_v,
    place_s,
    load_sem,
    place_sem,
    send_sem,
    recv_sem,
    msend_sem,
    mrecv_sem,
    hsend_sem,
    hrecv_sem,
    store_sem,
):
    levels, cells = x_v.shape
    tiles = cells // LANES
    blocks = blocks_v.shape[0]
    peers = dims[0] * dims[1] * dims[2]
    order = send_order(dims)
    section = lax.axis_index("sec")
    me = lax.axis_index("tile")
    other = 1 - section
    y, x, z = me // (dims[1] * dims[2]), (me // dims[2]) % dims[1], me % dims[2]

    def at(offset, sign):
        dy, dx, dz = offset
        ny, nx, nz = dims
        return (
            ((y + ny + sign * dy) % ny) * (nx * nz)
            + ((x + nx + sign * dx) % nx) * nz
            + (z + nz + sign * dz) % nz
        )

    after, before = (me + 1) % peers, (me + peers - 1) % peers

    start = other * (levels - FIELDS)
    get_export = pltpu.make_async_copy(state_hbm.at[pl.ds(start, FIELDS)], export_v, load_sem.at[0])
    get_export.start()
    chunks = 8
    per = blocks // chunks

    def get_blocks(c):
        part = pl.ds(c * per, per)
        return pltpu.make_async_copy(blocks_hbm.at[part], blocks_v.at[part], load_sem.at[1 + c])

    for c in range(chunks):
        get_blocks(c).start()

    barrier = pltpu.get_barrier_semaphore()
    for offset in order:
        pl.semaphore_signal(barrier, inc=1, device_id=(other, at(offset, -1)), device_id_type=MESH)
    for side in (before, after):
        pl.semaphore_signal(barrier, inc=1, device_id=(section, side), device_id_type=MESH)

    owner = dst_dev[...]
    earlier = lax.broadcasted_iota(jnp.int32, (blocks, blocks), 0) < lax.broadcasted_iota(
        jnp.int32, (blocks, blocks), 1
    )
    alike = earlier & (column(owner) == owner)
    position = owner * DEPTH + jnp.sum(jnp.where(alike, 1, 0), axis=0, keepdims=True)
    fills = column(position) == lax.broadcasted_iota(jnp.int32, (blocks, peers * DEPTH), 1)
    number = lax.broadcasted_iota(jnp.int32, (blocks, peers * DEPTH), 0)
    place_v[0:1, :] = jnp.sum(jnp.where(fills, number, 0), axis=0, keepdims=True)
    place_v[1:2, :] = jnp.sum(jnp.where(fills, column(dst_slot[...]) + 1, 0), axis=0, keepdims=True)
    get_place = pltpu.make_async_copy(place_v, place_s, place_sem)
    get_place.start()

    get_export.wait()
    for tile in range(tiles):
        cells_v[tile] = export_v[:, tile * LANES : (tile + 1) * LANES]

    def remap(c, carry):
        get_blocks(c).wait()
        for u in range(0, per, 2):
            b = c * per + u
            cell = jnp.concatenate([cells_v[src_slot[0, b]], cells_v[src_slot[0, b + 1]]], axis=0)
            both = lax.dot_general(
                cell.astype(jnp.bfloat16),
                blocks_v[pl.ds(b, 2)].reshape(2 * LANES, LANES),
                (((1,), (1,)), ((), ())),
                preferred_element_type=jnp.float32,
            )
            part_v[b] = both[:FIELDS, :LANES]
            part_v[b + 1] = both[FIELDS:, LANES:]
        return carry

    lax.fori_loop(0, chunks, remap, 0)
    get_state = pltpu.make_async_copy(state_hbm, x_v, load_sem.at[1 + chunks])
    get_state.start()
    get_place.wait()
    pl.semaphore_wait(barrier, peers + 2)

    rows = DEPTH * FIELDS
    lane = lax.broadcasted_iota(jnp.int32, (1, LANES), 1)
    group = LANES // DEPTH
    data, meta = [], []
    for k, offset in enumerate(order):
        dest = at(offset, 1)
        line = jnp.zeros((1, LANES), jnp.int32)
        for r in range(DEPTH):
            b = place_s[0, dest * DEPTH + r]
            out_v[pl.ds(k * rows + r * FIELDS, FIELDS), :] = part_v[b]
            line = jnp.where(lane == (k % group) * DEPTH + r, place_s[1, dest * DEPTH + r], line)
        meta_v[k] = line.astype(jnp.float32)
        target = (other, dest)
        copy = pltpu.make_async_remote_copy(
            src_ref=out_v.at[pl.ds(k * rows, rows)],
            dst_ref=recv_v.at[pl.ds(k * rows, rows)],
            send_sem=send_sem.at[k],
            recv_sem=recv_sem.at[k],
            device_id=target,
            device_id_type=MESH,
        )
        copy.start()
        data.append(copy)
        copy = pltpu.make_async_remote_copy(
            src_ref=meta_v.at[k],
            dst_ref=meta_r.at[k],
            send_sem=msend_sem.at[k],
            recv_sem=mrecv_sem.at[k],
            device_id=target,
            device_id_type=MESH,
        )
        copy.start()
        meta.append(copy)

    coef_v[...] = ring_powers()

    matrix = mats[section]
    full = weights(matrix)
    edge = weights(jnp.where(section == 0, matrix[:, levels - FIELDS :], matrix[:, :FIELDS]))
    width = 512
    get_state.wait()

    def ahead(i, carry):
        cols = pl.ds(pl.multiple_of(i * width, width), width)
        p_v[:, cols] = jnp.dot(full, stacked(x_v[:, cols]), preferred_element_type=jnp.float32)
        return carry

    lax.fori_loop(0, cells // width, ahead, 0)

    tile_number = lax.broadcasted_iota(jnp.int32, (tiles, LANES), 0).astype(jnp.float32)
    for q in range(peers // group):
        line = jnp.zeros((1, LANES), jnp.float32)
        for k in range(q * group, (q + 1) * group):
            meta[k].wait_recv()
            line = line + meta_r[k]
            data[k].wait_recv()
        chosen = (tile_number == line - 1.0).astype(jnp.float32)
        chosen = jnp.concatenate([chosen, chosen], axis=1).astype(jnp.bfloat16)
        for f in range(FIELDS):
            value = recv_v[pl.ds(q * group * rows + f, group * DEPTH, stride=FIELDS), :]
            high, low = split(value)
            term = jnp.dot(
                chosen,
                jnp.concatenate([high, low], axis=0).astype(jnp.bfloat16),
                preferred_element_type=jnp.float32,
            )
            to = pl.ds(f, tiles, stride=FIELDS)
            if q == 0:
                imp_v[to, :] = term
            else:
                imp_v[to, :] = imp_v[to, :] + term

    width = 2048
    chunks = cells // width
    per_width = width // LANES

    def columns(substeps, i, carry):
        i = (i + chunks - 1) % chunks
        cols = pl.ds(pl.multiple_of(i * width, width), width)
        imported = jnp.concatenate(
            [
                imp_v[pl.ds(pl.multiple_of((i * per_width + j) * FIELDS, FIELDS), FIELDS), :]
                for j in range(per_width)
            ],
            axis=1,
        )
        x_v[pl.ds(start, FIELDS), cols] = x_v[pl.ds(start, FIELDS), cols] + imported
        product = p_v[:, cols] + jnp.dot(edge, stacked(imported), preferred_element_type=jnp.float32)
        value = x_v[:, cols] + 0.5 * jnp.tanh(product)
        if substeps == 2:
            product = jnp.dot(full, stacked(value), preferred_element_type=jnp.float32)
            value = value + 0.5 * jnp.tanh(product)
        x_v[:, cols] = value
        return carry

    def physics(low, high):
        for number in range(2):

            @pl.when(section == number)
            def _(number=number):
                lax.fori_loop(low, high, functools.partial(columns, 2 - number), 0)

    physics(0, 2)
    halo = STEPS * LANES
    to_before = pltpu.make_async_remote_copy(
        src_ref=x_v.at[:, pl.ds(0, halo)],
        dst_ref=south_v,
        send_sem=hsend_sem.at[0],
        recv_sem=hrecv_sem.at[0],
        device_id=(section, before),
        device_id_type=MESH,
    )
    to_after = pltpu.make_async_remote_copy(
        src_ref=x_v.at[:, pl.ds(cells - halo, halo)],
        dst_ref=north_v,
        send_sem=hsend_sem.at[1],
        recv_sem=hrecv_sem.at[1],
        device_id=(section, after),
        device_id_type=MESH,
    )
    to_before.start()
    to_after.start()
    physics(2, chunks)

    rows_here = cells // LANES
    streams = 3
    bands = levels // (8 * streams)
    center, scale = viscosity(section)

    def level(low, s):
        return pl.ds(low + 8 * s if isinstance(low, int) else pl.multiple_of(low + 8 * s, 8), 8)

    def here(low, row):
        return [x_v[level(low, s), pl.ds(row * LANES, LANES)] for s in range(streams)]

    def keep(low, row, values):
        for s in range(streams):
            p_v[level(low, s), pl.ds((row + HALF) * LANES, LANES)] = values[s] * scale

    def inner(band):
        inside = pl.ds(2 * HALF * LANES, (rows_here - 2 * HALF) * LANES)
        span = pl.ds(pl.multiple_of(band * 8 * streams, 8), 8 * streams)
        return pltpu.make_async_copy(p_v.at[span, inside], out_hbm.at[span, inside], store_sem.at[band])

    def interior(band, carry):
        low = band * 8 * streams
        march(
            rows_here,
            16,
            streams,
            functools.partial(here, low),
            lambda row, values: keep(low, row - HALF, values),
            lambda row: None,
            coef_v,
            center,
        )
        inner(band).start()
        return carry

    lax.fori_loop(0, bands, interior, 0)

    for copy in (to_before, to_after):
        copy.wait()
    top = jnp.where(me == 0, 0.0, 1.0).astype(jnp.float32)
    bottom = jnp.where(me == peers - 1, 0.0, 1.0).astype(jnp.float32)
    edge_rows = 2 * STEPS
    for band in range(bands):
        low = band * 8 * streams

        def upper(row, low=low):
            if row >= STEPS:
                return here(low, row - STEPS)
            return [north_v[level(low, s), pl.ds(row * LANES, LANES)] for s in range(streams)]

        def lower(row, low=low):
            if row < STEPS:
                return here(low, rows_here - STEPS + row)
            return [south_v[level(low, s), pl.ds((row - STEPS) * LANES, LANES)] for s in range(streams)]

        march(
            edge_rows,
            edge_rows,
            streams,
            upper,
            lambda row, values, low=low: keep(low, row - STEPS - HALF, values),
            lambda row: top if row < STEPS else None,
            coef_v,
            center,
        )
        march(
            edge_rows,
            edge_rows,
            streams,
            lower,
            lambda row, values, low=low: keep(low, rows_here - STEPS + row - HALF, values),
            lambda row: bottom if row >= STEPS else None,
            coef_v,
            center,
        )
    stores = [inner(band) for band in range(bands)]
    for number, begin in enumerate((0, rows_here * LANES)):
        ends = pl.ds(begin, 2 * HALF * LANES)
        store = pltpu.make_async_copy(p_v.at[:, ends], out_hbm.at[:, ends], store_sem.at[bands + number])
        store.start()
        stores.append(store)
    for copy in data + meta:
        copy.wait_send()
    for store in stores:
        store.wait()


def ring_powers():
    shape = (2 * LANES, LANES)
    apart = (
        lax.broadcasted_iota(jnp.int32, shape, 0) + 2 * LANES - lax.broadcasted_iota(jnp.int32, shape, 1)
    ) % LANES
    terms = []
    for entries in ({1: 2}, {0: 2, 2: 1}):
        term = jnp.zeros(shape, jnp.float32)
        for distance, weight in entries.items():
            near = (apart == distance) | (apart == (LANES - distance) % LANES)
            term = jnp.where(near, float(weight), term)
        terms.append(term.astype(jnp.bfloat16))
    return jnp.concatenate(terms, axis=1)


def viscosity(section):
    visc = jnp.where(section == 0, ATMOS_VISC, OCEAN_VISC).astype(jnp.float32)
    return (1.0 - 4.0 * visc) / visc, visc * visc


def march(total, chunk, streams, load, emit, mask, coef_ref, center):
    def sides(row):
        value = jnp.concatenate([v for i in range(chunk) for v in load(row + i)], axis=0)
        high = value.astype(jnp.bfloat16)
        low = (value - high.astype(jnp.float32)).astype(jnp.bfloat16)
        return jnp.dot(
            jnp.concatenate([high, low], axis=1), coef_ref[...], preferred_element_type=jnp.float32
        )

    zero = jnp.zeros((8, LANES), jnp.float32)
    carry = [[(zero, zero) for _ in range(HALF)] for _ in range(streams)]
    late = [zero] * streams
    terms = sides(0)
    for begin in range(0, total, chunk):
        ahead = sides(begin + chunk) if begin + chunk < total else None
        for i in range(chunk):
            row = begin + i
            new = load(row)
            values = []
            for s in range(streams):
                m = (i * streams + s) * 8
                now = (terms[m : m + 8, :LANES], late[s])
                late[s] = terms[m : m + 8, LANES:]
                value = new[s]
                for k in range(HALF):
                    part, prior = carry[s][k]
                    factor = mask(row - k)
                    if factor is not None:
                        value = value * factor
                    carry[s][k] = (center * value + (now[k] + prior), value)
                    value = part + value
                values.append(value)
            if row >= 2 * HALF:
                emit(row, values)
        terms = ahead


def diffuse(x_hbm, o_hbm, x_v, o_v, coef_ref, get_sem, put_sem):
    levels, cells = x_v.shape
    rows = cells // LANES
    streams = 3
    bands = levels // (8 * streams)
    center, scale = viscosity(lax.axis_index("sec"))
    me = lax.axis_index("tile")
    top = jnp.where(me == 0, 0.0, 1.0).astype(jnp.float32)
    bottom = jnp.where(me == lax.axis_size("tile") - 1, 0.0, 1.0).astype(jnp.float32)

    def span(band):
        low = band * 8 * streams
        return pl.ds(low if isinstance(band, int) else pl.multiple_of(low, 8), 8 * streams)

    def get(band):
        return pltpu.make_async_copy(x_hbm.at[span(band)], x_v.at[span(band)], get_sem.at[band])

    def put(band):
        return pltpu.make_async_copy(o_v.at[span(band)], o_hbm.at[0, span(band)], put_sem.at[band])

    for band in range(bands):
        get(band).start()
    coef_ref[...] = ring_powers()

    def part(band, carry):
        low = band * 8 * streams

        def level(s):
            return pl.ds(pl.multiple_of(low + 8 * s, 8), 8)

        def load(row):
            return [x_v[level(s), pl.ds(row * LANES, LANES)] for s in range(streams)]

        def emit(row, values):
            for s in range(streams):
                o_v[level(s), pl.ds((row - 2 * HALF) * LANES, LANES)] = values[s] * scale

        def mask(row):
            return top if row < HALF else (bottom if row >= rows - HALF else None)

        get(band).wait()
        march(rows, 12, streams, load, emit, mask, coef_ref, center)
        put(band).start()
        return carry

    lax.fori_loop(0, bands, part, 0)
    for band in range(bands):
        put(band).wait()


def per_device(dims, section_state, matrices, blocks, src_slot, dst_dev, dst_slot):
    _, levels, cells = section_state.shape
    block_count = blocks.shape[1]
    tiles = cells // LANES
    peers = dims[0] * dims[1] * dims[2]
    halo = STEPS * LANES
    wide = cells + 2 * HALF * LANES
    f32, i32, dma = jnp.float32, jnp.int32, pltpu.SemaphoreType.DMA
    anywhere = pl.BlockSpec(memory_space=pl.ANY)
    vmem = pl.BlockSpec(memory_space=pltpu.VMEM)
    slots = peers * DEPTH * FIELDS
    state = pl.pallas_call(
        functools.partial(exchange, dims),
        out_shape=jax.ShapeDtypeStruct((levels, wide), f32),
        in_specs=[anywhere, vmem, anywhere, pl.BlockSpec(memory_space=pltpu.SMEM), vmem, vmem],
        out_specs=anywhere,
        scratch_shapes=[
            pltpu.VMEM((block_count, LANES, LANES), jnp.bfloat16),
            pltpu.VMEM((FIELDS, cells), f32),
            pltpu.VMEM((tiles, FIELDS, LANES), f32),
            pltpu.VMEM((block_count, FIELDS, LANES), f32),
            pltpu.VMEM((slots, LANES), f32),
            pltpu.VMEM((slots, LANES), f32),
            pltpu.VMEM((peers, 1, LANES), f32),
            pltpu.VMEM((peers, 1, LANES), f32),
            pltpu.VMEM((levels, cells), f32),
            pltpu.VMEM((levels, wide), f32),
            pltpu.VMEM((tiles * FIELDS, LANES), f32),
            pltpu.VMEM((levels, halo), f32),
            pltpu.VMEM((levels, halo), f32),
            pltpu.VMEM((2 * LANES, HALF * LANES), jnp.bfloat16),
            pltpu.VMEM((8, peers * DEPTH), i32),
            pltpu.SMEM((8, peers * DEPTH), i32),
            dma((10,)),
            dma,
            dma((peers,)),
            dma((peers,)),
            dma((peers,)),
            dma((peers,)),
            dma((2,)),
            dma((2,)),
            dma((8,)),
        ],
        compiler_params=pltpu.CompilerParams(
            collective_id=0, has_side_effects=True, vmem_limit_bytes=VMEM_BYTES
        ),
    )(
        section_state.reshape(levels, cells),
        matrices,
        blocks.reshape(block_count, LANES, LANES),
        src_slot,
        dst_dev.reshape(1, block_count),
        dst_slot,
    )
    return pl.pallas_call(
        diffuse,
        out_shape=jax.ShapeDtypeStruct((1, levels, cells), f32),
        in_specs=[anywhere],
        out_specs=anywhere,
        scratch_shapes=[
            pltpu.VMEM((levels, wide), f32),
            pltpu.VMEM((levels, cells), f32),
            pltpu.VMEM((2 * LANES, HALF * LANES), jnp.bfloat16),
            dma((8,)),
            dma((8,)),
        ],
        compiler_params=pltpu.CompilerParams(vmem_limit_bytes=VMEM_BYTES),
    )(state)


def solution(mesh):
    in_specs = (
        P("sec", None, "tile"),
        P(),
        P("sec", "tile", None, None),
        P("sec", "tile"),
        P("sec", "tile", None),
        P("sec", "tile"),
    )
    return jax.shard_map(
        functools.partial(per_device, torus(mesh.shape["tile"])),
        mesh=mesh,
        in_specs=in_specs,
        out_specs=P("sec", None, "tile"),
        check_vma=False,
    )
```

```python
import functools
import itertools
import random

import jax
import jax.numpy as jnp
from jax import lax
from jax.experimental import pallas as pl
from jax.experimental.pallas import tpu as pltpu
from jax.sharding import PartitionSpec as P

MESH = pl.DeviceIdType.MESH
FIELDS = 8
DEPTH = 8
LANES = 128
STEPS = 4
HALF = 2
ATMOS_VISC = 0.22
OCEAN_VISC = 0.24
VMEM_BYTES = 60 << 20


def torus(count):
    side = round(count ** (1 / 3))
    return (side, side, side)


def send_order(dims):
    offsets = list(itertools.product(*[range(n) for n in dims]))
    random.Random(1).shuffle(offsets)

    def hops(offset):
        return sum(min(a, n - a) for a, n in zip(offset, dims))

    return sorted(offsets, key=lambda offset: -hops(offset))


def split(value):
    high = value.astype(jnp.bfloat16).astype(jnp.float32)
    return high, value - high


def stacked(value):
    high, low = split(value)
    return jnp.concatenate([high, low, high], axis=0).astype(jnp.bfloat16)


def weights(matrix):
    high, low = split(matrix)
    return jnp.concatenate([high, high, low], axis=1).astype(jnp.bfloat16)


def column(row):
    return jnp.transpose(jnp.broadcast_to(row, (8, row.shape[1])))[:, :1]


def exchange(
    dims,
    state_hbm,
    mats,
    blocks_hbm,
    src_slot,
    dst_dev,
    dst_slot,
    out_hbm,
    blocks_v,
    export_v,
    cells_v,
    part_v,
    out_v,
    recv_v,
    meta_v,
    meta_r,
    x_v,
    p_v,
    imp_v,
    north_v,
    south_v,
    coef_v,
    place_v,
    place_s,
    load_sem,
    place_sem,
    send_sem,
    recv_sem,
    msend_sem,
    mrecv_sem,
    hsend_sem,
    hrecv_sem,
    store_sem,
):
    levels, cells = x_v.shape
    tiles = cells // LANES
    blocks = blocks_v.shape[0]
    peers = dims[0] * dims[1] * dims[2]
    order = send_order(dims)
    section = lax.axis_index("sec")
    me = lax.axis_index("tile")
    other = 1 - section
    y, x, z = me // (dims[1] * dims[2]), (me // dims[2]) % dims[1], me % dims[2]

    turn = 1 - 2 * section

    def at(offset, sign):
        dy, dx, dz = [sign * turn * a for a in offset]
        ny, nx, nz = dims
        return (
            ((y + ny + dy) % ny) * (nx * nz)
            + ((x + nx + dx) % nx) * nz
            + (z + nz + dz) % nz
        )

    after, before = (me + 1) % peers, (me + peers - 1) % peers

    start = other * (levels - FIELDS)
    get_export = pltpu.make_async_copy(state_hbm.at[pl.ds(start, FIELDS)], export_v, load_sem.at[0])
    get_export.start()
    chunks = 8
    per = blocks // chunks

    def get_blocks(c):
        part = pl.ds(c * per, per)
        return pltpu.make_async_copy(blocks_hbm.at[part], blocks_v.at[part], load_sem.at[1 + c])

    for c in range(chunks):
        get_blocks(c).start()

    barrier = pltpu.get_barrier_semaphore()
    for offset in order:
        pl.semaphore_signal(barrier, inc=1, device_id=(other, at(offset, 1)), device_id_type=MESH)
    for side in (before, after):
        pl.semaphore_signal(barrier, inc=1, device_id=(section, side), device_id_type=MESH)

    owner = dst_dev[...]
    earlier = lax.broadcasted_iota(jnp.int32, (blocks, blocks), 0) < lax.broadcasted_iota(
        jnp.int32, (blocks, blocks), 1
    )
    alike = earlier & (column(owner) == owner)
    position = owner * DEPTH + jnp.sum(jnp.where(alike, 1, 0), axis=0, keepdims=True)
    fills = column(position) == lax.broadcasted_iota(jnp.int32, (blocks, peers * DEPTH), 1)
    number = lax.broadcasted_iota(jnp.int32, (blocks, peers * DEPTH), 0)
    place_v[0:1, :] = jnp.sum(jnp.where(fills, number, 0), axis=0, keepdims=True)
    place_v[1:2, :] = jnp.sum(jnp.where(fills, column(dst_slot[...]) + 1, 0), axis=0, keepdims=True)
    get_place = pltpu.make_async_copy(place_v, place_s, place_sem)
    get_place.start()

    get_export.wait()
    for tile in range(tiles):
        cells_v[tile] = export_v[:, tile * LANES : (tile + 1) * LANES]

    def remap(c, carry):
        get_blocks(c).wait()
        for u in range(0, per, 2):
            b = c * per + u
            cell = jnp.concatenate([cells_v[src_slot[0, b]], cells_v[src_slot[0, b + 1]]], axis=0)
            both = lax.dot_general(
                cell.astype(jnp.bfloat16),
                blocks_v[pl.ds(b, 2)].reshape(2 * LANES, LANES),
                (((1,), (1,)), ((), ())),
                preferred_element_type=jnp.float32,
            )
            part_v[b] = both[:FIELDS, :LANES]
            part_v[b + 1] = both[FIELDS:, LANES:]
        return carry

    lax.fori_loop(0, chunks, remap, 0)
    get_state = pltpu.make_async_copy(state_hbm, x_v, load_sem.at[1 + chunks])
    get_state.start()
    get_place.wait()
    pl.semaphore_wait(barrier, peers + 2)

    rows = DEPTH * FIELDS
    lane = lax.broadcasted_iota(jnp.int32, (1, LANES), 1)
    group = LANES // DEPTH
    data, meta = [], []
    for k, offset in enumerate(order):
        dest = at(offset, 1)
        line = jnp.zeros((1, LANES), jnp.int32)
        for r in range(DEPTH):
            b = place_s[0, dest * DEPTH + r]
            out_v[pl.ds(k * rows + r * FIELDS, FIELDS), :] = part_v[b]
            line = jnp.where(lane == (k % group) * DEPTH + r, place_s[1, dest * DEPTH + r], line)
        meta_v[k] = line.astype(jnp.float32)
        target = (other, dest)
        copy = pltpu.make_async_remote_copy(
            src_ref=out_v.at[pl.ds(k * rows, rows)],
            dst_ref=recv_v.at[pl.ds(k * rows, rows)],
            send_sem=send_sem.at[k],
            recv_sem=recv_sem.at[k],
            device_id=target,
            device_id_type=MESH,
        )
        copy.start()
        data.append(copy)
        copy = pltpu.make_async_remote_copy(
            src_ref=meta_v.at[k],
            dst_ref=meta_r.at[k],
            send_sem=msend_sem.at[k],
            recv_sem=mrecv_sem.at[k],
            device_id=target,
            device_id_type=MESH,
        )
        copy.start()
        meta.append(copy)

    coef_v[...] = ring_powers()

    matrix = mats[section]
    full = weights(matrix)
    edge = weights(jnp.where(section == 0, matrix[:, levels - FIELDS :], matrix[:, :FIELDS]))
    width = 512
    get_state.wait()

    def ahead(i, carry):
        cols = pl.ds(pl.multiple_of(i * width, width), width)
        p_v[:, cols] = jnp.dot(full, stacked(x_v[:, cols]), preferred_element_type=jnp.float32)
        return carry

    lax.fori_loop(0, cells // width, ahead, 0)

    tile_number = lax.broadcasted_iota(jnp.int32, (tiles, LANES), 0).astype(jnp.float32)
    for q in range(peers // group):
        line = jnp.zeros((1, LANES), jnp.float32)
        for k in range(q * group, (q + 1) * group):
            meta[k].wait_recv()
            line = line + meta_r[k]
            data[k].wait_recv()
        chosen = (tile_number == line - 1.0).astype(jnp.float32)
        chosen = jnp.concatenate([chosen, chosen], axis=1).astype(jnp.bfloat16)
        for f in range(FIELDS):
            value = recv_v[pl.ds(q * group * rows + f, group * DEPTH, stride=FIELDS), :]
            high, low = split(value)
            term = jnp.dot(
                chosen,
                jnp.concatenate([high, low], axis=0).astype(jnp.bfloat16),
                preferred_element_type=jnp.float32,
            )
            to = pl.ds(f, tiles, stride=FIELDS)
            if q == 0:
                imp_v[to, :] = term
            else:
                imp_v[to, :] = imp_v[to, :] + term

    halo = STEPS * LANES
    width = 1536

    def rows_of(tile):
        return pl.ds(tile * FIELDS if isinstance(tile, int) else pl.multiple_of(tile * FIELDS, FIELDS), FIELDS)

    def columns(substeps, low, width):
        first = low // LANES
        if not isinstance(low, int):
            low = pl.multiple_of(low, LANES)
        cols = pl.ds(low, width)
        imported = jnp.concatenate(
            [imp_v[rows_of(first + j), :] for j in range(width // LANES)], axis=1
        )
        value = x_v[:, cols]
        if substeps == 2:
            value = jnp.concatenate([value[:-FIELDS], value[-FIELDS:] + imported], axis=0)
        else:
            value = jnp.concatenate([value[:FIELDS] + imported, value[FIELDS:]], axis=0)
        product = p_v[:, cols] + jnp.dot(edge, stacked(imported), preferred_element_type=jnp.float32)
        value = value + 0.5 * jnp.tanh(product)
        if substeps == 2:
            product = jnp.dot(full, stacked(value), preferred_element_type=jnp.float32)
            value = value + 0.5 * jnp.tanh(product)
        x_v[:, cols] = value

    for number in range(2):

        @pl.when(section == number)
        def _(number=number):
            columns(2 - number, 0, halo)
            columns(2 - number, cells - halo, halo)

    to_before = pltpu.make_async_remote_copy(
        src_ref=x_v.at[:, pl.ds(0, halo)],
        dst_ref=south_v,
        send_sem=hsend_sem.at[0],
        recv_sem=hrecv_sem.at[0],
        device_id=(section, before),
        device_id_type=MESH,
    )
    to_after = pltpu.make_async_remote_copy(
        src_ref=x_v.at[:, pl.ds(cells - halo, halo)],
        dst_ref=north_v,
        send_sem=hsend_sem.at[1],
        recv_sem=hrecv_sem.at[1],
        device_id=(section, after),
        device_id_type=MESH,
    )
    to_before.start()
    to_after.start()

    def middle(substeps, i, carry):
        columns(substeps, halo + i * width, width)
        return carry

    for number in range(2):

        @pl.when(section == number)
        def _(number=number):
            lax.fori_loop(0, (cells - 2 * halo) // width, functools.partial(middle, 2 - number), 0)

    rows_here = cells // LANES
    streams = 3
    bands = levels // (8 * streams)
    center, scale = viscosity(section)

    def level(low, s):
        return pl.ds(low + 8 * s if isinstance(low, int) else pl.multiple_of(low + 8 * s, 8), 8)

    def here(low, row):
        return [x_v[level(low, s), pl.ds(row * LANES, LANES)] for s in range(streams)]

    def keep(low, row, values):
        for s in range(streams):
            p_v[level(low, s), pl.ds((row + HALF) * LANES, LANES)] = values[s] * scale

    def inner(band):
        inside = pl.ds(2 * HALF * LANES, (rows_here - 2 * HALF) * LANES)
        span = pl.ds(pl.multiple_of(band * 8 * streams, 8), 8 * streams)
        return pltpu.make_async_copy(p_v.at[span, inside], out_hbm.at[span, inside], store_sem.at[band])

    def interior(band, carry):
        low = band * 8 * streams
        march(
            rows_here,
            16,
            streams,
            functools.partial(here, low),
            lambda row, values: keep(low, row - HALF, values),
            lambda row: None,
            coef_v,
            center,
        )
        inner(band).start()
        return carry

    lax.fori_loop(0, bands, interior, 0)

    for copy in (to_before, to_after):
        copy.wait()
    top = jnp.where(me == 0, 0.0, 1.0).astype(jnp.float32)
    bottom = jnp.where(me == peers - 1, 0.0, 1.0).astype(jnp.float32)
    edge_rows = 2 * STEPS
    for band in range(bands):
        low = band * 8 * streams

        def upper(row, low=low):
            if row >= STEPS:
                return here(low, row - STEPS)
            return [north_v[level(low, s), pl.ds(row * LANES, LANES)] for s in range(streams)]

        def lower(row, low=low):
            if row < STEPS:
                return here(low, rows_here - STEPS + row)
            return [south_v[level(low, s), pl.ds((row - STEPS) * LANES, LANES)] for s in range(streams)]

        march(
            edge_rows,
            edge_rows,
            streams,
            upper,
            lambda row, values, low=low: keep(low, row - STEPS - HALF, values),
            lambda row: top if row < STEPS else None,
            coef_v,
            center,
        )
        march(
            edge_rows,
            edge_rows,
            streams,
            lower,
            lambda row, values, low=low: keep(low, rows_here - STEPS + row - HALF, values),
            lambda row: bottom if row >= STEPS else None,
            coef_v,
            center,
        )
    stores = [inner(band) for band in range(bands)]
    for number, begin in enumerate((0, rows_here * LANES)):
        ends = pl.ds(begin, 2 * HALF * LANES)
        store = pltpu.make_async_copy(p_v.at[:, ends], out_hbm.at[:, ends], store_sem.at[bands + number])
        store.start()
        stores.append(store)
    for copy in data + meta:
        copy.wait_send()
    for store in stores:
        store.wait()


def ring_powers():
    shape = (2 * LANES, LANES)
    apart = (
        lax.broadcasted_iota(jnp.int32, shape, 0) + 2 * LANES - lax.broadcasted_iota(jnp.int32, shape, 1)
    ) % LANES
    terms = []
    for entries in ({1: 2}, {0: 2, 2: 1}):
        term = jnp.zeros(shape, jnp.float32)
        for distance, weight in entries.items():
            near = (apart == distance) | (apart == (LANES - distance) % LANES)
            term = jnp.where(near, float(weight), term)
        terms.append(term.astype(jnp.bfloat16))
    return jnp.concatenate(terms, axis=1)


def viscosity(section):
    visc = jnp.where(section == 0, ATMOS_VISC, OCEAN_VISC).astype(jnp.float32)
    return (1.0 - 4.0 * visc) / visc, visc * visc


def march(total, chunk, streams, load, emit, mask, coef_ref, center):
    def sides(row):
        value = jnp.concatenate([v for i in range(chunk) for v in load(row + i)], axis=0)
        high = value.astype(jnp.bfloat16)
        low = (value - high.astype(jnp.float32)).astype(jnp.bfloat16)
        return jnp.dot(
            jnp.concatenate([high, low], axis=1), coef_ref[...], preferred_element_type=jnp.float32
        )

    zero = jnp.zeros((8, LANES), jnp.float32)
    carry = [[(zero, zero) for _ in range(HALF)] for _ in range(streams)]
    late = [zero] * streams
    terms = sides(0)
    for begin in range(0, total, chunk):
        ahead = sides(begin + chunk) if begin + chunk < total else None
        for i in range(chunk):
            row = begin + i
            new = load(row)
            values = []
            for s in range(streams):
                m = (i * streams + s) * 8
                now = (terms[m : m + 8, :LANES], late[s])
                late[s] = terms[m : m + 8, LANES:]
                value = new[s]
                for k in range(HALF):
                    part, prior = carry[s][k]
                    factor = mask(row - k)
                    if factor is not None:
                        value = value * factor
                    carry[s][k] = (center * value + (now[k] + prior), value)
                    value = part + value
                values.append(value)
            if row >= 2 * HALF:
                emit(row, values)
        terms = ahead


def diffuse(x_hbm, o_hbm, x_v, o_v, coef_ref, get_sem, put_sem):
    levels, cells = x_v.shape
    rows = cells // LANES
    streams = 3
    bands = levels // (8 * streams)
    center, scale = viscosity(lax.axis_index("sec"))
    me = lax.axis_index("tile")
    top = jnp.where(me == 0, 0.0, 1.0).astype(jnp.float32)
    bottom = jnp.where(me == lax.axis_size("tile") - 1, 0.0, 1.0).astype(jnp.float32)

    def span(band):
        low = band * 8 * streams
        return pl.ds(low if isinstance(band, int) else pl.multiple_of(low, 8), 8 * streams)

    def get(band):
        return pltpu.make_async_copy(x_hbm.at[span(band)], x_v.at[span(band)], get_sem.at[band])

    def put(band):
        return pltpu.make_async_copy(o_v.at[span(band)], o_hbm.at[0, span(band)], put_sem.at[band])

    for band in range(bands):
        get(band).start()
    coef_ref[...] = ring_powers()

    def part(band, carry):
        low = band * 8 * streams

        def level(s):
            return pl.ds(pl.multiple_of(low + 8 * s, 8), 8)

        def load(row):
            return [x_v[level(s), pl.ds(row * LANES, LANES)] for s in range(streams)]

        def emit(row, values):
            for s in range(streams):
                o_v[level(s), pl.ds((row - 2 * HALF) * LANES, LANES)] = values[s] * scale

        def mask(row):
            return top if row < HALF else (bottom if row >= rows - HALF else None)

        get(band).wait()
        march(rows, 12, streams, load, emit, mask, coef_ref, center)
        put(band).start()
        return carry

    lax.fori_loop(0, bands, part, 0)
    for band in range(bands):
        put(band).wait()


def per_device(dims, section_state, matrices, blocks, src_slot, dst_dev, dst_slot):
    _, levels, cells = section_state.shape
    block_count = blocks.shape[1]
    tiles = cells // LANES
    peers = dims[0] * dims[1] * dims[2]
    halo = STEPS * LANES
    wide = cells + 2 * HALF * LANES
    f32, i32, dma = jnp.float32, jnp.int32, pltpu.SemaphoreType.DMA
    anywhere = pl.BlockSpec(memory_space=pl.ANY)
    vmem = pl.BlockSpec(memory_space=pltpu.VMEM)
    slots = peers * DEPTH * FIELDS
    state = pl.pallas_call(
        functools.partial(exchange, dims),
        out_shape=jax.ShapeDtypeStruct((levels, wide), f32),
        in_specs=[anywhere, vmem, anywhere, pl.BlockSpec(memory_space=pltpu.SMEM), vmem, vmem],
        out_specs=anywhere,
        scratch_shapes=[
            pltpu.VMEM((block_count, LANES, LANES), jnp.bfloat16),
            pltpu.VMEM((FIELDS, cells), f32),
            pltpu.VMEM((tiles, FIELDS, LANES), f32),
            pltpu.VMEM((block_count, FIELDS, LANES), f32),
            pltpu.VMEM((slots, LANES), f32),
            pltpu.VMEM((slots, LANES), f32),
            pltpu.VMEM((peers, 1, LANES), f32),
            pltpu.VMEM((peers, 1, LANES), f32),
            pltpu.VMEM((levels, cells), f32),
            pltpu.VMEM((levels, wide), f32),
            pltpu.VMEM((tiles * FIELDS, LANES), f32),
            pltpu.VMEM((levels, halo), f32),
            pltpu.VMEM((levels, halo), f32),
            pltpu.VMEM((2 * LANES, HALF * LANES), jnp.bfloat16),
            pltpu.VMEM((8, peers * DEPTH), i32),
            pltpu.SMEM((8, peers * DEPTH), i32),
            dma((10,)),
            dma,
            dma((peers,)),
            dma((peers,)),
            dma((peers,)),
            dma((peers,)),
            dma((2,)),
            dma((2,)),
            dma((8,)),
        ],
        compiler_params=pltpu.CompilerParams(
            collective_id=0, has_side_effects=True, vmem_limit_bytes=VMEM_BYTES
        ),
    )(
        section_state.reshape(levels, cells),
        matrices,
        blocks.reshape(block_count, LANES, LANES),
        src_slot,
        dst_dev.reshape(1, block_count),
        dst_slot,
    )
    return pl.pallas_call(
        diffuse,
        out_shape=jax.ShapeDtypeStruct((1, levels, cells), f32),
        in_specs=[anywhere],
        out_specs=anywhere,
        scratch_shapes=[
            pltpu.VMEM((levels, wide), f32),
            pltpu.VMEM((levels, cells), f32),
            pltpu.VMEM((2 * LANES, HALF * LANES), jnp.bfloat16),
            dma((8,)),
            dma((8,)),
        ],
        compiler_params=pltpu.CompilerParams(vmem_limit_bytes=VMEM_BYTES),
    )(state)


def solution(mesh):
    in_specs = (
        P("sec", None, "tile"),
        P(),
        P("sec", "tile", None, None),
        P("sec", "tile"),
        P("sec", "tile", None),
        P("sec", "tile"),
    )
    return jax.shard_map(
        functools.partial(per_device, torus(mesh.shape["tile"])),
        mesh=mesh,
        in_specs=in_specs,
        out_specs=P("sec", None, "tile"),
        check_vma=False,
    )
```

```python
import functools
import itertools
import random

import jax
import jax.numpy as jnp
from jax import lax
from jax.experimental import pallas as pl
from jax.experimental.pallas import tpu as pltpu
from jax.sharding import PartitionSpec as P

MESH = pl.DeviceIdType.MESH
FIELDS = 8
DEPTH = 8
LANES = 128
STEPS = 4
HALF = 2
ATMOS_VISC = 0.22
OCEAN_VISC = 0.24
VMEM_BYTES = 60 << 20


def torus(count):
    side = round(count ** (1 / 3))
    return (side, side, side)


def send_order(dims):
    offsets = list(itertools.product(*[range(n) for n in dims]))
    random.Random(1).shuffle(offsets)

    def hops(offset):
        return sum(min(a, n - a) for a, n in zip(offset, dims))

    return sorted(offsets, key=lambda offset: -hops(offset) - 0.5 * min(offset[2], dims[2] - offset[2]))


def split(value):
    high = value.astype(jnp.bfloat16).astype(jnp.float32)
    return high, value - high


def stacked(value):
    high, low = split(value)
    return jnp.concatenate([high, low, high], axis=0).astype(jnp.bfloat16)


def weights(matrix):
    high, low = split(matrix)
    return jnp.concatenate([high, high, low], axis=1).astype(jnp.bfloat16)


def column(row):
    return jnp.transpose(jnp.broadcast_to(row, (8, row.shape[1])))[:, :1]


def exchange(
    dims,
    state_hbm,
    mats,
    blocks_hbm,
    src_slot,
    dst_dev,
    dst_slot,
    out_hbm,
    blocks_v,
    export_v,
    cells_v,
    part_v,
    out_v,
    recv_v,
    meta_v,
    meta_r,
    x_v,
    p_v,
    imp_v,
    north_v,
    south_v,
    coef_v,
    place_v,
    place_s,
    load_sem,
    place_sem,
    send_sem,
    recv_sem,
    msend_sem,
    mrecv_sem,
    hsend_sem,
    hrecv_sem,
    store_sem,
):
    levels, cells = x_v.shape
    tiles = cells // LANES
    blocks = blocks_v.shape[0]
    peers = dims[0] * dims[1] * dims[2]
    order = send_order(dims)
    section = lax.axis_index("sec")
    me = lax.axis_index("tile")
    other = 1 - section
    y, x, z = me // (dims[1] * dims[2]), (me // dims[2]) % dims[1], me % dims[2]

    turn = 1 - 2 * section

    def at(offset, sign):
        dy, dx, dz = [sign * turn * a for a in offset]
        ny, nx, nz = dims
        return (
            ((y + ny + dy) % ny) * (nx * nz)
            + ((x + nx + dx) % nx) * nz
            + (z + nz + dz) % nz
        )

    after, before = (me + 1) % peers, (me + peers - 1) % peers

    start = other * (levels - FIELDS)
    get_export = pltpu.make_async_copy(state_hbm.at[pl.ds(start, FIELDS)], export_v, load_sem.at[0])
    get_export.start()
    chunks = 8
    per = blocks // chunks

    def get_blocks(c):
        part = pl.ds(c * per, per)
        return pltpu.make_async_copy(blocks_hbm.at[part], blocks_v.at[part], load_sem.at[1 + c])

    for c in range(chunks):
        get_blocks(c).start()

    barrier = pltpu.get_barrier_semaphore()
    for offset in order:
        pl.semaphore_signal(barrier, inc=1, device_id=(other, at(offset, 1)), device_id_type=MESH)
    for side in (before, after):
        pl.semaphore_signal(barrier, inc=1, device_id=(section, side), device_id_type=MESH)

    owner = dst_dev[...]
    earlier = lax.broadcasted_iota(jnp.int32, (blocks, blocks), 0) < lax.broadcasted_iota(
        jnp.int32, (blocks, blocks), 1
    )
    alike = earlier & (column(owner) == owner)
    position = owner * DEPTH + jnp.sum(jnp.where(alike, 1, 0), axis=0, keepdims=True)
    fills = column(position) == lax.broadcasted_iota(jnp.int32, (blocks, peers * DEPTH), 1)
    number = lax.broadcasted_iota(jnp.int32, (blocks, peers * DEPTH), 0)
    place_v[0:1, :] = jnp.sum(jnp.where(fills, number, 0), axis=0, keepdims=True)
    place_v[1:2, :] = jnp.sum(jnp.where(fills, column(dst_slot[...]) + 1, 0), axis=0, keepdims=True)
    get_place = pltpu.make_async_copy(place_v, place_s, place_sem)
    get_place.start()

    get_export.wait()
    for tile in range(tiles):
        cells_v[tile] = export_v[:, tile * LANES : (tile + 1) * LANES]

    def remap(c, carry):
        get_blocks(c).wait()
        for u in range(0, per, 2):
            b = c * per + u
            cell = jnp.concatenate([cells_v[src_slot[0, b]], cells_v[src_slot[0, b + 1]]], axis=0)
            both = lax.dot_general(
                cell.astype(jnp.bfloat16),
                blocks_v[pl.ds(b, 2)].reshape(2 * LANES, LANES),
                (((1,), (1,)), ((), ())),
                preferred_element_type=jnp.float32,
            )
            part_v[b] = both[:FIELDS, :LANES]
            part_v[b + 1] = both[FIELDS:, LANES:]
        return carry

    lax.fori_loop(0, chunks, remap, 0)
    get_state = pltpu.make_async_copy(state_hbm, x_v, load_sem.at[1 + chunks])
    get_state.start()
    get_place.wait()
    pl.semaphore_wait(barrier, peers + 2)

    rows = DEPTH * FIELDS
    lane = lax.broadcasted_iota(jnp.int32, (1, LANES), 1)
    group = LANES // DEPTH
    data, meta = [], []
    for k, offset in enumerate(order):
        dest = at(offset, 1)
        line = jnp.zeros((1, LANES), jnp.int32)
        for r in range(DEPTH):
            b = place_s[0, dest * DEPTH + r]
            out_v[pl.ds(k * rows + r * FIELDS, FIELDS), :] = part_v[b]
            line = jnp.where(lane == (k % group) * DEPTH + r, place_s[1, dest * DEPTH + r], line)
        meta_v[k] = line.astype(jnp.float32)
        target = (other, dest)
        copy = pltpu.make_async_remote_copy(
            src_ref=out_v.at[pl.ds(k * rows, rows)],
            dst_ref=recv_v.at[pl.ds(k * rows, rows)],
            send_sem=send_sem.at[k],
            recv_sem=recv_sem.at[k],
            device_id=target,
            device_id_type=MESH,
        )
        copy.start()
        data.append(copy)
        copy = pltpu.make_async_remote_copy(
            src_ref=meta_v.at[k],
            dst_ref=meta_r.at[k],
            send_sem=msend_sem.at[k],
            recv_sem=mrecv_sem.at[k],
            device_id=target,
            device_id_type=MESH,
        )
        copy.start()
        meta.append(copy)

    coef_v[...] = ring_powers()

    matrix = mats[section]
    full = weights(matrix)
    edge = weights(jnp.where(section == 0, matrix[:, levels - FIELDS :], matrix[:, :FIELDS]))
    width = 512
    get_state.wait()

    def ahead(i, carry):
        cols = pl.ds(pl.multiple_of(i * width, width), width)
        p_v[:, cols] = jnp.dot(full, stacked(x_v[:, cols]), preferred_element_type=jnp.float32)
        return carry

    lax.fori_loop(0, cells // width, ahead, 0)

    tile_number = lax.broadcasted_iota(jnp.int32, (tiles, LANES), 0).astype(jnp.float32)
    for q in range(peers // group):
        line = jnp.zeros((1, LANES), jnp.float32)
        for k in range(q * group, (q + 1) * group):
            meta[k].wait_recv()
            line = line + meta_r[k]
            data[k].wait_recv()
        chosen = (tile_number == line - 1.0).astype(jnp.float32)
        chosen = jnp.concatenate([chosen, chosen], axis=1).astype(jnp.bfloat16)
        for f in range(FIELDS):
            value = recv_v[pl.ds(q * group * rows + f, group * DEPTH, stride=FIELDS), :]
            high, low = split(value)
            term = jnp.dot(
                chosen,
                jnp.concatenate([high, low], axis=0).astype(jnp.bfloat16),
                preferred_element_type=jnp.float32,
            )
            to = pl.ds(f, tiles, stride=FIELDS)
            if q == 0:
                imp_v[to, :] = term
            else:
                imp_v[to, :] = imp_v[to, :] + term

    halo = STEPS * LANES
    width = 1536

    def rows_of(tile):
        return pl.ds(tile * FIELDS if isinstance(tile, int) else pl.multiple_of(tile * FIELDS, FIELDS), FIELDS)

    def columns(substeps, low, width):
        first = low // LANES
        if not isinstance(low, int):
            low = pl.multiple_of(low, LANES)
        cols = pl.ds(low, width)
        imported = jnp.concatenate(
            [imp_v[rows_of(first + j), :] for j in range(width // LANES)], axis=1
        )
        value = x_v[:, cols]
        if substeps == 2:
            value = jnp.concatenate([value[:-FIELDS], value[-FIELDS:] + imported], axis=0)
        else:
            value = jnp.concatenate([value[:FIELDS] + imported, value[FIELDS:]], axis=0)
        product = p_v[:, cols] + jnp.dot(edge, stacked(imported), preferred_element_type=jnp.float32)
        value = value + 0.5 * jnp.tanh(product)
        if substeps == 2:
            product = jnp.dot(full, stacked(value), preferred_element_type=jnp.float32)
            value = value + 0.5 * jnp.tanh(product)
        x_v[:, cols] = value

    for number in range(2):

        @pl.when(section == number)
        def _(number=number):
            columns(2 - number, 0, halo)
            columns(2 - number, cells - halo, halo)

    to_before = pltpu.make_async_remote_copy(
        src_ref=x_v.at[:, pl.ds(0, halo)],
        dst_ref=south_v,
        send_sem=hsend_sem.at[0],
        recv_sem=hrecv_sem.at[0],
        device_id=(section, before),
        device_id_type=MESH,
    )
    to_after = pltpu.make_async_remote_copy(
        src_ref=x_v.at[:, pl.ds(cells - halo, halo)],
        dst_ref=north_v,
        send_sem=hsend_sem.at[1],
        recv_sem=hrecv_sem.at[1],
        device_id=(section, after),
        device_id_type=MESH,
    )
    to_before.start()
    to_after.start()

    def middle(substeps, i, carry):
        columns(substeps, halo + i * width, width)
        return carry

    for number in range(2):

        @pl.when(section == number)
        def _(number=number):
            lax.fori_loop(0, (cells - 2 * halo) // width, functools.partial(middle, 2 - number), 0)

    rows_here = cells // LANES
    streams = 3
    bands = levels // (8 * streams)
    center, scale = viscosity(section)

    def level(low, s):
        return pl.ds(low + 8 * s if isinstance(low, int) else pl.multiple_of(low + 8 * s, 8), 8)

    def here(low, row):
        return [x_v[level(low, s), pl.ds(row * LANES, LANES)] for s in range(streams)]

    def keep(low, row, values):
        for s in range(streams):
            p_v[level(low, s), pl.ds((row + HALF) * LANES, LANES)] = values[s] * scale

    def inner(band):
        inside = pl.ds(2 * HALF * LANES, (rows_here - 2 * HALF) * LANES)
        span = pl.ds(pl.multiple_of(band * 8 * streams, 8), 8 * streams)
        return pltpu.make_async_copy(p_v.at[span, inside], out_hbm.at[span, inside], store_sem.at[band])

    def interior(band, carry):
        low = band * 8 * streams
        march(
            rows_here,
            16,
            streams,
            functools.partial(here, low),
            lambda row, values: keep(low, row - HALF, values),
            lambda row: None,
            coef_v,
            center,
        )
        inner(band).start()
        return carry

    lax.fori_loop(0, bands, interior, 0)

    for copy in (to_before, to_after):
        copy.wait()
    top = jnp.where(me == 0, 0.0, 1.0).astype(jnp.float32)
    bottom = jnp.where(me == peers - 1, 0.0, 1.0).astype(jnp.float32)
    edge_rows = 2 * STEPS
    for band in range(bands):
        low = band * 8 * streams

        def upper(row, low=low):
            if row >= STEPS:
                return here(low, row - STEPS)
            return [north_v[level(low, s), pl.ds(row * LANES, LANES)] for s in range(streams)]

        def lower(row, low=low):
            if row < STEPS:
                return here(low, rows_here - STEPS + row)
            return [south_v[level(low, s), pl.ds((row - STEPS) * LANES, LANES)] for s in range(streams)]

        march(
            edge_rows,
            edge_rows,
            streams,
            upper,
            lambda row, values, low=low: keep(low, row - STEPS - HALF, values),
            lambda row: top if row < STEPS else None,
            coef_v,
            center,
        )
        march(
            edge_rows,
            edge_rows,
            streams,
            lower,
            lambda row, values, low=low: keep(low, rows_here - STEPS + row - HALF, values),
            lambda row: bottom if row >= STEPS else None,
            coef_v,
            center,
        )
    stores = [inner(band) for band in range(bands)]
    for number, begin in enumerate((0, rows_here * LANES)):
        ends = pl.ds(begin, 2 * HALF * LANES)
        store = pltpu.make_async_copy(p_v.at[:, ends], out_hbm.at[:, ends], store_sem.at[bands + number])
        store.start()
        stores.append(store)
    for copy in data + meta:
        copy.wait_send()
    for store in stores:
        store.wait()


def ring_powers():
    shape = (2 * LANES, LANES)
    apart = (
        lax.broadcasted_iota(jnp.int32, shape, 0) + 2 * LANES - lax.broadcasted_iota(jnp.int32, shape, 1)
    ) % LANES
    terms = []
    for entries in ({1: 2}, {0: 2, 2: 1}):
        term = jnp.zeros(shape, jnp.float32)
        for distance, weight in entries.items():
            near = (apart == distance) | (apart == (LANES - distance) % LANES)
            term = jnp.where(near, float(weight), term)
        terms.append(term.astype(jnp.bfloat16))
    return jnp.concatenate(terms, axis=1)


def viscosity(section):
    visc = jnp.where(section == 0, ATMOS_VISC, OCEAN_VISC).astype(jnp.float32)
    return (1.0 - 4.0 * visc) / visc, visc * visc


def march(total, chunk, streams, load, emit, mask, coef_ref, center):
    def sides(row):
        value = jnp.concatenate([v for i in range(chunk) for v in load(row + i)], axis=0)
        high = value.astype(jnp.bfloat16)
        low = (value - high.astype(jnp.float32)).astype(jnp.bfloat16)
        return jnp.dot(
            jnp.concatenate([high, low], axis=1), coef_ref[...], preferred_element_type=jnp.float32
        )

    zero = jnp.zeros((8, LANES), jnp.float32)
    carry = [[(zero, zero) for _ in range(HALF)] for _ in range(streams)]
    late = [zero] * streams
    terms = sides(0)
    for begin in range(0, total, chunk):
        ahead = sides(begin + chunk) if begin + chunk < total else None
        for i in range(chunk):
            row = begin + i
            new = load(row)
            values = []
            for s in range(streams):
                m = (i * streams + s) * 8
                now = (terms[m : m + 8, :LANES], late[s])
                late[s] = terms[m : m + 8, LANES:]
                value = new[s]
                for k in range(HALF):
                    part, prior = carry[s][k]
                    factor = mask(row - k)
                    if factor is not None:
                        value = value * factor
                    carry[s][k] = (center * value + (now[k] + prior), value)
                    value = part + value
                values.append(value)
            if row >= 2 * HALF:
                emit(row, values)
        terms = ahead


def diffuse(x_hbm, o_hbm, x_v, o_v, coef_ref, get_sem, put_sem):
    levels, cells = x_v.shape
    rows = cells // LANES
    streams = 3
    bands = levels // (8 * streams)
    center, scale = viscosity(lax.axis_index("sec"))
    me = lax.axis_index("tile")
    top = jnp.where(me == 0, 0.0, 1.0).astype(jnp.float32)
    bottom = jnp.where(me == lax.axis_size("tile") - 1, 0.0, 1.0).astype(jnp.float32)

    def span(band):
        low = band * 8 * streams
        return pl.ds(low if isinstance(band, int) else pl.multiple_of(low, 8), 8 * streams)

    def get(band):
        return pltpu.make_async_copy(x_hbm.at[span(band)], x_v.at[span(band)], get_sem.at[band])

    def put(band):
        return pltpu.make_async_copy(o_v.at[span(band)], o_hbm.at[0, span(band)], put_sem.at[band])

    for band in range(bands):
        get(band).start()
    coef_ref[...] = ring_powers()

    def part(band, carry):
        low = band * 8 * streams

        def level(s):
            return pl.ds(pl.multiple_of(low + 8 * s, 8), 8)

        def load(row):
            return [x_v[level(s), pl.ds(row * LANES, LANES)] for s in range(streams)]

        def emit(row, values):
            for s in range(streams):
                o_v[level(s), pl.ds((row - 2 * HALF) * LANES, LANES)] = values[s] * scale

        def mask(row):
            return top if row < HALF else (bottom if row >= rows - HALF else None)

        get(band).wait()
        march(rows, 12, streams, load, emit, mask, coef_ref, center)
        put(band).start()
        return carry

    lax.fori_loop(0, bands, part, 0)
    for band in range(bands):
        put(band).wait()


def per_device(dims, section_state, matrices, blocks, src_slot, dst_dev, dst_slot):
    _, levels, cells = section_state.shape
    block_count = blocks.shape[1]
    tiles = cells // LANES
    peers = dims[0] * dims[1] * dims[2]
    halo = STEPS * LANES
    wide = cells + 2 * HALF * LANES
    f32, i32, dma = jnp.float32, jnp.int32, pltpu.SemaphoreType.DMA
    anywhere = pl.BlockSpec(memory_space=pl.ANY)
    vmem = pl.BlockSpec(memory_space=pltpu.VMEM)
    slots = peers * DEPTH * FIELDS
    state = pl.pallas_call(
        functools.partial(exchange, dims),
        out_shape=jax.ShapeDtypeStruct((levels, wide), f32),
        in_specs=[anywhere, vmem, anywhere, pl.BlockSpec(memory_space=pltpu.SMEM), vmem, vmem],
        out_specs=anywhere,
        scratch_shapes=[
            pltpu.VMEM((block_count, LANES, LANES), jnp.bfloat16),
            pltpu.VMEM((FIELDS, cells), f32),
            pltpu.VMEM((tiles, FIELDS, LANES), f32),
            pltpu.VMEM((block_count, FIELDS, LANES), f32),
            pltpu.VMEM((slots, LANES), f32),
            pltpu.VMEM((slots, LANES), f32),
            pltpu.VMEM((peers, 1, LANES), f32),
            pltpu.VMEM((peers, 1, LANES), f32),
            pltpu.VMEM((levels, cells), f32),
            pltpu.VMEM((levels, wide), f32),
            pltpu.VMEM((tiles * FIELDS, LANES), f32),
            pltpu.VMEM((levels, halo), f32),
            pltpu.VMEM((levels, halo), f32),
            pltpu.VMEM((2 * LANES, HALF * LANES), jnp.bfloat16),
            pltpu.VMEM((8, peers * DEPTH), i32),
            pltpu.SMEM((8, peers * DEPTH), i32),
            dma((10,)),
            dma,
            dma((peers,)),
            dma((peers,)),
            dma((peers,)),
            dma((peers,)),
            dma((2,)),
            dma((2,)),
            dma((8,)),
        ],
        compiler_params=pltpu.CompilerParams(
            collective_id=0, has_side_effects=True, vmem_limit_bytes=VMEM_BYTES
        ),
    )(
        section_state.reshape(levels, cells),
        matrices,
        blocks.reshape(block_count, LANES, LANES),
        src_slot,
        dst_dev.reshape(1, block_count),
        dst_slot,
    )
    return pl.pallas_call(
        diffuse,
        out_shape=jax.ShapeDtypeStruct((1, levels, cells), f32),
        in_specs=[anywhere],
        out_specs=anywhere,
        scratch_shapes=[
            pltpu.VMEM((levels, wide), f32),
            pltpu.VMEM((levels, cells), f32),
            pltpu.VMEM((2 * LANES, HALF * LANES), jnp.bfloat16),
            dma((8,)),
            dma((8,)),
        ],
        compiler_params=pltpu.CompilerParams(vmem_limit_bytes=VMEM_BYTES),
    )(state)


def solution(mesh):
    in_specs = (
        P("sec", None, "tile"),
        P(),
        P("sec", "tile", None, None),
        P("sec", "tile"),
        P("sec", "tile", None),
        P("sec", "tile"),
    )
    return jax.shard_map(
        functools.partial(per_device, torus(mesh.shape["tile"])),
        mesh=mesh,
        in_specs=in_specs,
        out_specs=P("sec", None, "tile"),
        check_vma=False,
    )
```
